128 devices in a mesh: group: 8 (over z_hi, x), domain: 16 (over y, z_lo, core).
Axes of the slice: x: 4, y: 4, z: 4 (z_hi: 2, z_lo: 2; z = z_hi * 2 + z_lo), core: 2. Of those that a mesh axis runs over, the one named last changes fastest.
Arguments:
- weight: float32 [8192, 7168], P(('group', 'domain')), may hold values from -6 to 6
- moment1: float32 [8192, 7168], P(('group', 'domain')), may hold values from -4 to 4
- moment2: float32 [8192, 7168], P(('group', 'domain')), may hold values from 0.01 to 1
- gradient: bfloat16 [8192, 7168], P(('group', 'domain')), may hold values from -6 to 6
- owner_table: int32 [16, 8], replicated, may hold values from 0 to 7, each once within a row
- exponents: int32 [8], replicated, may hold values from 0 to 7, each once
Outputs:
- weight_new: float32 [8192, 7168], P(('group', 'domain'))
- moment1_new: float32 [8192, 7168], P(('group', 'domain'))
- moment2_new: float32 [8192, 7168], P(('group', 'domain'))
- buddy_copy: float32 [8192, 3, 7168], P(('group', 'domain'))
- parity: float32 [1024, 3, 7168], P(('group', 'domain'))
The draws below stay inside these ranges and needn't reach their ends.
Inputs may be any that keep to these rules, and one draw needn't show every extreme that they name: Each row of owner_table names every member once. `exponents`: every member has a different exponent.
All inputs are finite; a program needn't handle non-finite values.
Results may differ from the reference program's by a relative error of at most 0.0003.
Values sent between devices are 32-bit elements; how exact they have to be, the bound alone decides.
A program may use at most 128 MiB of HBM per device.

```python
import math
import jax
import jax.numpy as jnp
from jax import lax

D = 7168
ROWS_DEV = 64
MEMBERS = 8
DOMAINS = 16
STRIDE = 4
STRIPE = 8
ROWS = 8192


def level_of(key, dims, pieces, least, top_value):
    def one(axis_at, parts):
        steps = jax.random.uniform(jax.random.fold_in(jax.random.fold_in(key, 6), axis_at), (parts,), jnp.float32, least / len(pieces), top_value / len(pieces))
        return jnp.repeat(jnp.exp(steps), dims[axis_at] // parts).reshape((-1,) + (1,) * (len(dims) - axis_at - 1))

    level = one(*pieces[0])
    for cut in pieces[1:]:
        level = level * one(*cut)
    return level


def normal_values(rng, dims, width, bound, cuts=(), dtype=jnp.bfloat16):
    entries = width * jax.random.normal(rng, dims, jnp.float32)
    if cuts:
        entries = entries * level_of(rng, dims, cuts, -0.22, 0.18)
    return jnp.clip(entries, -bound, bound).astype(dtype)


def setup_inputs(seed: int = 0) -> dict:
    splits = jax.random.split(jax.random.key(seed), 7)
    weight = normal_values(splits[0], (ROWS, D), 1.0, 6.0, ((0, 128),), jnp.float32)
    moment1 = normal_values(splits[1], (ROWS, D), 0.5, 4.0, ((0, 128),), jnp.float32)
    moment2 = jnp.clip(jnp.exp(math.log(1.0) - 4.6051702 * jax.random.uniform(splits[2], (ROWS, D), jnp.float32) ** level_of(splits[2], (ROWS, D), ((0, 128),), -0.2, 0.2)), 0.01, 1.0)
    gradient = normal_values(splits[3], (ROWS, D), 1.0, 6.0, ((0, 128),))
    owner_table = jax.vmap(lambda own: jax.random.permutation(own, MEMBERS))(jax.random.split(splits[4], DOMAINS)).reshape((DOMAINS, MEMBERS)).astype(jnp.int32)
    exponents = jax.random.permutation(splits[5], MEMBERS).astype(jnp.int32)
    return {"weight": weight, "moment1": moment1, "moment2": moment2, "gradient": gradient, "owner_table": owner_table, "exponents": exponents}


beta_one = 0.9
beta_two = 0.95
learning_rate = 0.02
weight_decay = 0.1
epsilon = 1e-08
step_count = 100.0

def adamw(weight, moment1, moment2, gradient):
    grad_float = gradient.astype(jnp.float32)
    first = beta_one * moment1 + (1.0 - beta_one) * grad_float
    second = beta_two * moment2 + (1.0 - beta_two) * grad_float * grad_float
    correct_one = 1.0 - beta_one ** step_count
    correct_two = 1.0 - beta_two ** step_count
    update = first / correct_one / (jnp.sqrt(second / correct_two) + epsilon) + weight_decay * weight
    return (weight - learning_rate * update, first, second)

def reference(weight, moment1, moment2, gradient, owner_table, exponents):
    weight_new, moment1_new, moment2_new = adamw(weight, moment1, moment2, gradient)
    packed = jnp.stack([weight_new, moment1_new, moment2_new], axis=1)
    blocks = packed.reshape(MEMBERS, DOMAINS, ROWS_DEV, 3, D)
    buddy_copy = jnp.roll(blocks, STRIDE, axis=1).reshape(ROWS, 3, D)
    stripes = blocks.reshape(MEMBERS, DOMAINS, MEMBERS, STRIPE, 3, D)
    points = 1.0 + (2.0 * jnp.arange(MEMBERS).astype(jnp.float32) + 1.0 - MEMBERS) / (4.0 * MEMBERS)
    coef = jnp.power(points[None, :], exponents.astype(jnp.float32)[:, None])
    summed = jnp.einsum('ks,kdsrcn->dsrcn', coef, stripes, precision=lax.Precision.HIGHEST)
    inverse = jnp.argsort(owner_table, axis=1).astype(jnp.int32)
    domain_ids = jnp.arange(DOMAINS).astype(jnp.int32)[None, :]
    chosen = summed[domain_ids, inverse.T]
    parity = chosen.reshape(ROWS // MEMBERS, 3, D)
    return (weight_new, moment1_new, moment2_new, buddy_copy, parity)
```

```python
import functools

import jax
import jax.numpy as jnp
from jax import lax
from jax.experimental import pallas as pl
from jax.experimental.pallas import tpu as pltpu
from jax.sharding import PartitionSpec as P

beta_one = 0.9
beta_two = 0.95
learning_rate = 0.02
weight_decay = 0.1
epsilon = 1e-08
step_count = 100.0

MESH = pl.DeviceIdType.MESH
XS, ZHS, YS, ZLS, CORES = 4, 2, 4, 2, 2
STRIPE = 8
LONG_STRIPES = 2


def adamw(weight, moment1, moment2, gradient):
    grad_float = gradient.astype(jnp.float32)
    first = beta_one * moment1 + (1.0 - beta_one) * grad_float
    second = beta_two * moment2 + (1.0 - beta_two) * grad_float * grad_float
    correct_one = 1.0 - beta_one**step_count
    correct_two = 1.0 - beta_two**step_count
    update = (
        first / correct_one / (jnp.sqrt(second / correct_two) + epsilon) + weight_decay * weight
    )
    return (weight - learning_rate * update, first, second)


def coefficient(stripe, exponent):
    bits = [(jnp.right_shift(exponent, i) & 1).astype(jnp.float32) for i in range(3)]
    point = 1.0 + (2.0 * stripe.astype(jnp.float32) - 7.0) / 32.0
    square = point * point
    fourth = square * square
    power = 1.0
    for bit, factor in zip(bits, (point, square, fourth)):
        power = power * (1.0 + bit * (factor - 1.0))
    return power


def same(a, b):
    gap = a - b
    return 1 - jnp.minimum(jnp.maximum(gap, -gap), 1)


def exchange_kernel(
    owner_ref, exponent_ref, w_ref, m_ref, v_ref, buddy_ref, parity_ref,
    held, scaled, arrived, total, hop1, hop2,
    load_sem, plus_send, plus_recv, hop_send, hop_recv, piece_send, piece_recv, out_sem,
):
    group = lax.axis_index("group")
    domain = lax.axis_index("domain")
    x = group % XS
    zh = group // XS
    per_y = ZLS * CORES
    y_plus = (domain + per_y) % (YS * per_y)
    y_minus = (domain + (YS - 1) * per_y) % (YS * per_y)
    arrays = (w_ref, m_ref, v_ref)
    stripes = w_ref.shape[0]
    short = stripes - LONG_STRIPES

    offsets = [(dx, dz) for dz in range(ZHS) for dx in range(XS)]
    partners = [((zh + dz) % ZHS) * XS + (x + dx) % XS for dx, dz in offsets]

    loads = []
    for a in range(3):
        load = pltpu.make_async_copy(arrays[a], held.at[a], load_sem.at[a])
        load.start()
        loads.append(load)

    barrier = pltpu.get_barrier_semaphore()
    for other in (y_plus, y_minus):
        pl.semaphore_signal(barrier, inc=1, device_id=(group, other), device_id_type=MESH)
    for partner in partners[1:]:
        pl.semaphore_signal(barrier, inc=1, device_id=(partner, domain), device_id_type=MESH)
    pl.semaphore_wait(barrier, 2 + len(partners) - 1)

    plus = []
    for a in range(3):
        copy = pltpu.make_async_remote_copy(
            src_ref=arrays[a].at[pl.ds(0, short)],
            dst_ref=buddy_ref.at[a, pl.ds(0, short)],
            send_sem=plus_send.at[a],
            recv_sem=plus_recv.at[a],
            device_id=(group, y_plus),
            device_id_type=MESH,
        )
        copy.start()
        plus.append(copy)

    chunks = [(a, r) for r in range(LONG_STRIPES) for a in range(3)]

    def hop(step, i):
        a, r = chunks[i]
        source = (arrays[a].at[short + r], hop1.at[i], hop2.at[i])[step]
        target = (hop1.at[i], hop2.at[i], buddy_ref.at[a, short + r])[step]
        return pltpu.make_async_remote_copy(
            src_ref=source,
            dst_ref=target,
            send_sem=hop_send.at[step, i],
            recv_sem=hop_recv.at[step, i],
            device_id=(group, y_minus),
            device_id_type=MESH,
        )

    for i in range(len(chunks)):
        hop(0, i).start()

    exponent = exponent_ref[group]
    for load in loads:
        load.wait()

    def stripe_of(owner):
        stripe = jnp.int32(0)
        for s in range(stripes):
            stripe = stripe + s * same(owner_ref[domain, s], owner)
        return jnp.minimum(stripe, stripes - 1)

    pieces = []
    for slot in [1, 3, 4, 2, 5, 7, 6, 0]:
        stripe = stripe_of(partners[slot])
        scale = coefficient(stripe, exponent)
        for a in range(3):
            scaled[slot, a] = held[a, stripe] * scale
        if slot:
            piece = pltpu.make_async_remote_copy(
                src_ref=scaled.at[slot],
                dst_ref=arrived.at[slot - 1],
                send_sem=piece_send.at[slot - 1],
                recv_sem=piece_recv.at[slot - 1],
                device_id=(partners[slot], domain),
                device_id_type=MESH,
            )
            piece.start()
            pieces.append(piece)

    for step in range(2):
        for i in range(len(chunks)):
            hop(step, i).wait_recv()
            hop(step + 1, i).start()

    total[...] = scaled[0]
    for slot, piece in zip([1, 3, 4, 2, 5, 7, 6], pieces):
        piece.wait_recv()
        total[...] += arrived[slot - 1]
    out = pltpu.make_async_copy(total, parity_ref, out_sem)
    out.start()

    for i in range(len(chunks)):
        hop(2, i).wait_recv()
    for copy in plus:
        copy.wait()
    for step in range(3):
        for i in range(len(chunks)):
            hop(step, i).wait_send()
    for piece in pieces:
        piece.wait_send()
    out.wait()


def exchange(owner_table, exponents, w, m, v):
    members = XS * ZHS
    stripes, width = w.shape[0] // STRIPE, w.shape[1]
    chunks = 3 * LONG_STRIPES
    w, m, v = (a.reshape(stripes, STRIPE, width) for a in (w, m, v))
    smem = pl.BlockSpec(memory_space=pltpu.SMEM)
    anywhere = pl.BlockSpec(memory_space=pl.ANY)
    f32 = jnp.float32
    dma = pltpu.SemaphoreType.DMA
    return pl.pallas_call(
        exchange_kernel,
        out_shape=(
            jax.ShapeDtypeStruct((3, stripes, STRIPE, width), f32),
            jax.ShapeDtypeStruct((3, STRIPE, width), f32),
        ),
        in_specs=[smem, smem, anywhere, anywhere, anywhere],
        out_specs=(anywhere, anywhere),
        scratch_shapes=[
            pltpu.VMEM((3, stripes, STRIPE, width), f32),
            pltpu.VMEM((members, 3, STRIPE, width), f32),
            pltpu.VMEM((members - 1, 3, STRIPE, width), f32),
            pltpu.VMEM((3, STRIPE, width), f32),
            pltpu.VMEM((chunks, STRIPE, width), f32),
            pltpu.VMEM((chunks, STRIPE, width), f32),
            dma((3,)),
            dma((3,)),
            dma((3,)),
            dma((3, chunks)),
            dma((3, chunks)),
            dma((members - 1,)),
            dma((members - 1,)),
            dma,
        ],
        compiler_params=pltpu.CompilerParams(
            collective_id=0, has_side_effects=True, vmem_limit_bytes=40 << 20
        ),
        name="exchange",
    )(owner_table, exponents, w, m, v)


def shards(weight, moment1, moment2, gradient, owner_table, exponents):
    w, m, v = adamw(weight, moment1, moment2, gradient)
    buddy, parity = exchange(owner_table, exponents, w, m, v)
    buddy = buddy.reshape(3, -1, buddy.shape[-1])
    return (w, m, v, jnp.transpose(buddy, (1, 0, 2)), jnp.transpose(parity, (1, 0, 2)))


def solution(mesh):
    rows = P(("group", "domain"), None)
    blocks = P(("group", "domain"), None, None)
    return jax.shard_map(
        shards,
        mesh=mesh,
        in_specs=(rows, rows, rows, rows, P(), P()),
        out_specs=(rows, rows, rows, blocks, blocks),
        check_vma=False,
    )
```

```python
import jax
import jax.numpy as jnp
from jax import lax
from jax.experimental import pallas as pl
from jax.experimental.pallas import tpu as pltpu
from jax.sharding import PartitionSpec as P

beta_one = 0.9
beta_two = 0.95
learning_rate = 0.02
weight_decay = 0.1
epsilon = 1e-08
step_count = 100.0

MESH = pl.DeviceIdType.MESH
XS, ZS, YS, ZLS, CORES = 4, 4, 4, 2, 2
ZHS = ZS // ZLS
STRIPE = 8
LONG_STRIPES = 2
F32 = jnp.float32
DMA = pltpu.SemaphoreType.DMA
IN_HBM = pl.BlockSpec(memory_space=pltpu.HBM)
IN_VMEM = pl.BlockSpec(memory_space=pltpu.VMEM)


def adamw(weight, moment1, moment2, gradient):
    grad_float = gradient.astype(F32)
    first = beta_one * moment1 + (1.0 - beta_one) * grad_float
    second = beta_two * moment2 + (1.0 - beta_two) * grad_float * grad_float
    correct_one = 1.0 - beta_one**step_count
    correct_two = 1.0 - beta_two**step_count
    update = (
        first / correct_one / (jnp.sqrt(second / correct_two) + epsilon) + weight_decay * weight
    )
    return (weight - learning_rate * update, first, second)


def coefficient(stripe, exponent):
    bits = [(jnp.right_shift(exponent, i) & 1).astype(F32) for i in range(3)]
    point = 1.0 + (2.0 * stripe.astype(F32) - 7.0) / 32.0
    square = point * point
    fourth = square * square
    power = 1.0
    for bit, factor in zip(bits, (point, square, fourth)):
        power = power * (1.0 + bit * (factor - 1.0))
    return power


def same(a, b):
    gap = a - b
    return 1 - jnp.minimum(jnp.maximum(gap, -gap), 1)


def exchange_kernel(
    owners_in, exponents_in, w_in, m_in, v_in, g_in, fresh, buddy_ref, parity_ref,
    w, m, v, g, owner_ref, exponent_ref, scaled, first_in, second_in, relay, across, hop1, hop2,
    load_sem, table_sem, plus_send, plus_recv, hop_send, hop_recv, x_send, x_recv, z_send, z_recv,
):
    group = lax.axis_index("group")
    domain = lax.axis_index("domain")
    x, zh = group % XS, group // XS
    core, zl, y = domain % CORES, (domain // CORES) % ZLS, domain // (CORES * ZLS)
    z = zh * ZLS + zl

    def device(x, y, z):
        return ((z // ZLS) * XS + x, (y * ZLS + z % ZLS) * CORES + core)

    y_plus, y_minus = device(x, (y + 1) % YS, z), device(x, (y + YS - 1) % YS, z)
    x_plus, x_minus = device((x + 1) % XS, y, z), device((x + XS - 1) % XS, y, z)
    z_plus, z_minus = device(x, y, (z + 1) % ZS), device(x, y, (z + ZS - 1) % ZS)
    stripes = w.shape[0]
    short = stripes - LONG_STRIPES
    half = w.shape[2] // 2

    tables = [
        pltpu.make_async_copy(owners_in, owner_ref, table_sem.at[0]),
        pltpu.make_async_copy(exponents_in, exponent_ref, table_sem.at[1]),
    ]

    def loads(pair):
        two, rows = pl.ds(2 * pair, 2), pl.ds(2 * STRIPE * pair, 2 * STRIPE)
        ends = [(w_in.at[two], w.at[two]), (m_in.at[two], m.at[two]), (v_in.at[two], v.at[two])]
        ends.append((g_in.at[rows], g.at[rows]))
        return [pltpu.make_async_copy(*e, load_sem.at[pair, i]) for i, e in enumerate(ends)]

    pairs = [stripes // 2 - 1, *range(stripes // 2 - 1)]
    for pair in pairs:
        for load in loads(pair):
            load.start()

    def send(source, target, send_sem, recv_sem, to):
        return pltpu.make_async_remote_copy(
            src_ref=source,
            dst_ref=target,
            send_sem=send_sem,
            recv_sem=recv_sem,
            device_id=to,
            device_id_type=MESH,
        )

    barrier = pltpu.get_barrier_semaphore()
    neighbours = (y_plus, y_minus, x_plus, x_minus, z_plus, z_minus)
    for other in neighbours:
        pl.semaphore_signal(barrier, inc=1, device_id=other, device_id_type=MESH)
    for table in tables:
        table.start()

    def update(pair):
        for load in loads(pair):
            load.wait()
        gradient = g[pl.ds(2 * STRIPE * pair, 2 * STRIPE), :].astype(F32)
        for h in range(2):
            s = 2 * pair + h
            fresh[0, s], fresh[1, s], fresh[2, s] = adamw(
                w[s], m[s], v[s], gradient[h * STRIPE : (h + 1) * STRIPE]
            )

    def plus(s):
        return send(fresh.at[:, s], buddy_ref.at[:, s], plus_send.at[s], plus_recv.at[s], y_plus)

    chunks = [(a, short + r) for r in range(LONG_STRIPES) for a in range(3)]

    def hop(step, i):
        a, s = chunks[i]
        source = (fresh.at[a, s], hop1.at[i], hop2.at[i])[step]
        target = (hop1.at[i], hop2.at[i], buddy_ref.at[a, s])[step]
        return send(source, target, hop_send.at[step, i], hop_recv.at[step, i], y_minus)

    update(pairs[0])
    update(pairs[1])
    pl.semaphore_wait(barrier, len(neighbours))
    for i in range(len(chunks)):
        hop(0, i).start()
        if i < 2:
            plus(2 * pairs[1] + i).start()
    for pair in pairs[2:]:
        update(pair)
        plus(2 * pair).start()
        plus(2 * pair + 1).start()

    for table in tables:
        table.wait()
    exponent = exponent_ref[group]

    def scale(dx, dz):
        owner = ((zh + dz) % ZHS) * XS + (x + dx) % XS
        stripe = jnp.int32(0)
        for s in range(stripes):
            stripe = stripe + s * same(owner_ref[s, domain], owner)
        stripe = jnp.minimum(stripe, stripes - 1)
        factor = coefficient(stripe, exponent)
        for a in range(3):
            scaled[dz * XS + dx, a] = fresh[a, stripe] * factor

    def along_x(i, slot, target, to):
        return send(scaled.at[slot], target, x_send.at[i], x_recv.at[i], to)

    far_plus = along_x(0, 2, first_in.at[0], x_plus)
    far_minus = along_x(1, XS + 2, first_in.at[1], x_minus)
    near_plus = along_x(2, XS + 1, second_in.at[0], x_plus)
    near_minus = along_x(3, XS - 1, second_in.at[1], x_minus)
    sum_plus = along_x(4, 1, second_in.at[2], x_plus)
    sum_minus = along_x(5, XS + XS - 1, second_in.at[3], x_minus)
    scale(2, 0)
    far_plus.start()
    scale(2, 1)
    far_minus.start()
    scale(1, 1)
    near_plus.start()
    scale(3, 0)
    near_minus.start()
    scale(1, 0)
    scale(3, 1)
    scale(0, 0)
    scale(0, 1)

    far_plus.wait_recv()
    scaled[1] += first_in[0]
    sum_plus.start()
    far_minus.wait_recv()
    scaled[XS + XS - 1] += first_in[1]
    sum_minus.start()

    for i in range(len(chunks)):
        hop(0, i).wait_recv()
        hop(1, i).start()

    for copy in (near_plus, near_minus, sum_plus, sum_minus):
        copy.wait_recv()
    scaled[XS] += second_in[0] + second_in[3]
    left, right = pl.ds(0, half), pl.ds(half, half)
    out_plus = send(scaled.at[XS, :, :, left], relay.at[0], z_send.at[0], z_recv.at[0], z_plus)
    out_minus = send(scaled.at[XS, :, :, right], relay.at[1], z_send.at[1], z_recv.at[1], z_minus)
    on_plus = send(relay.at[0], across.at[0], z_send.at[2], z_recv.at[2], z_plus)
    on_minus = send(relay.at[1], across.at[1], z_send.at[3], z_recv.at[3], z_minus)
    out_plus.start()
    out_minus.start()
    parity_ref[...] = scaled[0] + second_in[1] + second_in[2]
    out_plus.wait_recv()
    on_plus.start()
    out_minus.wait_recv()
    on_minus.start()

    for i in range(len(chunks)):
        hop(1, i).wait_recv()
        hop(2, i).start()

    on_plus.wait_recv()
    parity_ref[:, :, left] += across[0]
    on_minus.wait_recv()
    parity_ref[:, :, right] += across[1]

    for copy in (far_plus, far_minus, near_plus, near_minus, sum_plus, sum_minus):
        copy.wait_send()
    for copy in (out_plus, out_minus, on_plus, on_minus):
        copy.wait_send()
    for step in range(3):
        for i in range(len(chunks)):
            hop(step, i).wait_send()
    for s in range(short):
        plus(s).wait_send()
    for s in range(short):
        plus(s).wait_recv()
    for i in range(len(chunks)):
        hop(2, i).wait_recv()


def exchange(owners, exponents, w, m, v, g):
    shape = w.shape
    stripes, _, width = shape
    chunks = 3 * LONG_STRIPES
    block = (3, STRIPE, width)
    halves = (2, 3, STRIPE, width // 2)
    return pl.pallas_call(
        exchange_kernel,
        out_shape=(
            pltpu.VMEM((3, *shape), F32),
            pltpu.VMEM((3, *shape), F32),
            pltpu.VMEM(block, F32),
        ),
        in_specs=[IN_HBM] * 6,
        out_specs=(IN_VMEM,) * 3,
        scratch_shapes=[
            pltpu.VMEM(shape, F32),
            pltpu.VMEM(shape, F32),
            pltpu.VMEM(shape, F32),
            pltpu.VMEM(g.shape, g.dtype),
            pltpu.SMEM(owners.shape, jnp.int32),
            pltpu.SMEM(exponents.shape, jnp.int32),
            pltpu.VMEM((XS * ZHS, *block), F32),
            pltpu.VMEM((2, *block), F32),
            pltpu.VMEM((4, *block), F32),
            pltpu.VMEM(halves, F32),
            pltpu.VMEM(halves, F32),
            pltpu.VMEM((chunks, STRIPE, width), F32),
            pltpu.VMEM((chunks, STRIPE, width), F32),
            DMA((stripes // 2, 4)),
            DMA((2,)),
            DMA((stripes,)),
            DMA((stripes,)),
            DMA((3, chunks)),
            DMA((3, chunks)),
            DMA((6,)),
            DMA((6,)),
            DMA((4,)),
            DMA((4,)),
        ],
        compiler_params=pltpu.CompilerParams(
            collective_id=0, has_side_effects=True, vmem_limit_bytes=40 << 20
        ),
        name="exchange",
    )(owners, exponents, w, m, v, g)


def finish_kernel(fresh, buddy, parity, w_out, m_out, v_out, buddy_out, parity_out, sem):
    copies = [pltpu.make_async_copy(parity, parity_out, sem.at[0])]
    for a, out in enumerate((w_out, m_out, v_out)):
        copies.append(pltpu.make_async_copy(fresh.at[a], out, sem.at[1 + a]))
        copies.append(pltpu.make_async_copy(buddy.at[a], buddy_out.at[a], sem.at[4 + a]))
    for copy in copies:
        copy.start()
    for copy in copies:
        copy.wait()


def finish(fresh, buddy, parity):
    one = jax.ShapeDtypeStruct(fresh.shape[1:], F32)
    return pl.pallas_call(
        finish_kernel,
        out_shape=(
            one,
            one,
            one,
            jax.ShapeDtypeStruct(buddy.shape, F32),
            jax.ShapeDtypeStruct(parity.shape, F32),
        ),
        in_specs=[IN_VMEM] * 3,
        out_specs=(IN_HBM,) * 5,
        scratch_shapes=[DMA((7,))],
        compiler_params=pltpu.CompilerParams(vmem_limit_bytes=1 << 20),
        name="finish",
    )(fresh, buddy, parity)


def shards(weight, moment1, moment2, gradient, owner_table, exponents):
    rows, width = weight.shape
    w, m, v = (a.reshape(rows // STRIPE, STRIPE, width) for a in (weight, moment1, moment2))
    held = (owner_table.T, exponents, w, m, v, gradient)
    held = (pltpu.with_memory_space_constraint(a, pltpu.HBM) for a in held)
    fresh, buddy, parity = exchange(*held)
    w, m, v, buddy, parity = finish(fresh, buddy, parity)
    buddy = jnp.transpose(buddy.reshape(3, rows, width), (1, 0, 2))
    parity = jnp.transpose(parity, (1, 0, 2))
    return (*(a.reshape(rows, width) for a in (w, m, v)), buddy, parity)


def solution(mesh):
    rows = P(("group", "domain"), None)
    blocks = P(("group", "domain"), None, None)
    return jax.shard_map(
        shards,
        mesh=mesh,
        in_specs=(rows, rows, rows, rows, P(), P()),
        out_specs=(rows, rows, rows, blocks, blocks),
        check_vma=False,
    )
```

```python
import jax
import jax.numpy as jnp
from jax import lax
from jax.experimental import pallas as pl
from jax.experimental.pallas import tpu as pltpu
from jax.sharding import PartitionSpec as P

beta_one = 0.9
beta_two = 0.95
learning_rate = 0.02
weight_decay = 0.1
epsilon = 1e-08
step_count = 100.0

MESH = pl.DeviceIdType.MESH
XS, ZS, YS, ZLS, CORES = 4, 4, 4, 2, 2
ZHS = ZS // ZLS
STRIPE = 8
PARTS = 4
CUTS = 2
F32 = jnp.float32
DMA = pltpu.SemaphoreType.DMA
IN_HBM = pl.BlockSpec(memory_space=pltpu.HBM)
IN_VMEM = pl.BlockSpec(memory_space=pltpu.VMEM)


def adamw(weight, moment1, moment2, gradient):
    grad_float = gradient.astype(F32)
    first = beta_one * moment1 + (1.0 - beta_one) * grad_float
    second = beta_two * moment2 + (1.0 - beta_two) * grad_float * grad_float
    correct_one = 1.0 - beta_one**step_count
    correct_two = 1.0 - beta_two**step_count
    update = (
        first / correct_one / (jnp.sqrt(second / correct_two) + epsilon) + weight_decay * weight
    )
    return (weight - learning_rate * update, first, second)


def coefficient(stripe, exponent):
    bits = [(jnp.right_shift(exponent, i) & 1).astype(F32) for i in range(3)]
    point = 1.0 + (2.0 * stripe.astype(F32) - 7.0) / 32.0
    square = point * point
    fourth = square * square
    power = 1.0
    for bit, factor in zip(bits, (point, square, fourth)):
        power = power * (1.0 + bit * (factor - 1.0))
    return power


def same(a, b):
    gap = a - b
    return 1 - jnp.minimum(jnp.maximum(gap, -gap), 1)


def exchange_kernel(
    owners_in, exponents_in, w_in, m_in, v_in, g_in, fresh, buddy_ref, parity_ref,
    w, m, v, g, owner_ref, exponent_ref, scaled, first_in, second_in, relay, across, hop1, hop2,
    load_sem, table_sem, plus_send, plus_recv, hop_send, hop_recv, x_send, x_recv, z_send, z_recv,
):
    group = lax.axis_index("group")
    domain = lax.axis_index("domain")
    x, zh = group % XS, group // XS
    core, zl, y = domain % CORES, (domain // CORES) % ZLS, domain // (CORES * ZLS)
    z = zh * ZLS + zl

    def device(x, y, z):
        return ((z // ZLS) * XS + x, (y * ZLS + z % ZLS) * CORES + core)

    y_plus, y_minus = device(x, (y + 1) % YS, z), device(x, (y + YS - 1) % YS, z)
    x_plus, x_minus = device((x + 1) % XS, y, z), device((x + XS - 1) % XS, y, z)
    z_plus, z_minus = device(x, y, (z + 1) % ZS), device(x, y, (z + ZS - 1) % ZS)
    stripes = w.shape[0]
    half = w.shape[2] // 2
    part = w.shape[2] // PARTS

    tables = [
        pltpu.make_async_copy(owners_in, owner_ref, table_sem.at[0]),
        pltpu.make_async_copy(exponents_in, exponent_ref, table_sem.at[1]),
    ]

    first, last = 0, stripes // 2 - 1
    blocks = [
        (first, 0, part),
        (last, 0, part),
        (first, part, half * 2 - part),
        (last, part, half * 2 - part),
    ]
    blocks += [(pair, 0, half * 2) for pair in range(first + 1, last)]

    def loads(b):
        pair, start, size = blocks[b]
        two, rows, columns = pl.ds(2 * pair, 2), pl.ds(2 * STRIPE * pair, 2 * STRIPE), pl.ds(start, size)
        ends = [(src.at[two, :, columns], dst.at[two, :, columns]) for src, dst in ((w_in, w), (m_in, m), (v_in, v))]
        ends.append((g_in.at[rows, columns], g.at[rows, columns]))
        return [pltpu.make_async_copy(*e, load_sem.at[b, i]) for i, e in enumerate(ends)]

    for b in range(len(blocks)):
        for load in loads(b):
            load.start()

    def send(source, target, send_sem, recv_sem, to):
        return pltpu.make_async_remote_copy(
            src_ref=source,
            dst_ref=target,
            send_sem=send_sem,
            recv_sem=recv_sem,
            device_id=to,
            device_id_type=MESH,
        )

    barrier = pltpu.get_barrier_semaphore()
    beside, along_z = (y_plus, y_minus, x_plus, x_minus), (z_plus, z_minus)

    def greet(others):
        for other in others:
            pl.semaphore_signal(barrier, inc=1, device_id=other, device_id_type=MESH)

    greet(beside)

    def meet():
        @pl.when(zl == 0)
        def _():
            pl.semaphore_wait(barrier, len(beside))
            greet(along_z)

        @pl.when(zl == 1)
        def _():
            pl.semaphore_wait(barrier, len(beside) + len(along_z))
            greet(along_z)

    def meet_along_z():
        @pl.when(zl == 0)
        def _():
            pl.semaphore_wait(barrier, len(along_z))

    def update(b):
        pair, start, size = blocks[b]
        columns = pl.ds(start, size)
        for load in loads(b):
            load.wait()
        gradient = g[pl.ds(2 * STRIPE * pair, 2 * STRIPE), columns].astype(F32)
        for h in range(2):
            s = 2 * pair + h
            new = adamw(
                w[s, :, columns], m[s, :, columns], v[s, :, columns],
                gradient[h * STRIPE : (h + 1) * STRIPE],
            )
            for a in range(3):
                fresh[a, s, :, columns] = new[a]

    def plus(b):
        pair, start, size = blocks[b]
        here = (slice(None), pl.ds(2 * pair, 2), slice(None), pl.ds(start, size))
        return send(fresh.at[here], buddy_ref.at[here], plus_send.at[b], plus_recv.at[b], y_plus)

    def hop(step, i):
        here = (slice(None), pl.ds(2 * last, 2), slice(None), pl.ds(i * part, part))
        source = (fresh.at[here], hop1.at[i], hop2.at[i])[step]
        target = (hop1.at[i], hop2.at[i], buddy_ref.at[here])[step]
        return send(source, target, hop_send.at[step, i], hop_recv.at[step, i], y_minus)

    short = [b for b in range(len(blocks)) if blocks[b][0] != last]

    update(0)
    meet()
    plus(0).start()
    for table in tables:
        table.start()
    update(1)
    hop(0, 0).start()
    update(2)
    plus(2).start()
    update(3)
    for i in range(1, PARTS):
        hop(0, i).start()
    for b in short[2:]:
        update(b)
        plus(b).start()

    for table in tables:
        table.wait()
    exponent = exponent_ref[group]

    def scale(dx, dz):
        owner = ((zh + dz) % ZHS) * XS + (x + dx) % XS
        stripe = jnp.int32(0)
        for s in range(stripes):
            stripe = stripe + s * same(owner_ref[s, domain], owner)
        stripe = jnp.minimum(stripe, stripes - 1)
        factor = coefficient(stripe, exponent)
        for a in range(3):
            scaled[dz * XS + dx, a] = fresh[a, stripe] * factor

    def along_x(i, slot, target, to):
        return send(scaled.at[slot], target, x_send.at[i], x_recv.at[i], to)

    far_plus = along_x(0, 2, first_in.at[0], x_plus)
    far_minus = along_x(1, XS + 2, first_in.at[1], x_minus)
    near_plus = along_x(2, XS + 1, second_in.at[0], x_plus)
    near_minus = along_x(3, XS - 1, second_in.at[1], x_minus)
    sum_plus = along_x(4, 1, second_in.at[2], x_plus)
    sum_minus = along_x(5, XS + XS - 1, second_in.at[3], x_minus)
    scale(2, 0)
    far_plus.start()
    scale(2, 1)
    far_minus.start()
    scale(1, 1)
    near_plus.start()
    scale(3, 0)
    near_minus.start()
    scale(1, 0)
    scale(3, 1)
    scale(0, 0)
    scale(0, 1)

    far_plus.wait_recv()
    scaled[1] += first_in[0]
    sum_plus.start()
    far_minus.wait_recv()
    scaled[XS + XS - 1] += first_in[1]
    sum_minus.start()

    for i in range(PARTS):
        hop(0, i).wait_recv()
        hop(1, i).start()

    for copy in (near_plus, near_minus, sum_plus, sum_minus):
        copy.wait_recv()
    scaled[XS] += second_in[0] + second_in[3]
    left, right = pl.ds(0, half), pl.ds(half, half)
    out_plus = send(scaled.at[XS, :, :, left], relay.at[0], z_send.at[0], z_recv.at[0], z_plus)
    out_minus = send(scaled.at[XS, :, :, right], relay.at[1], z_send.at[1], z_recv.at[1], z_minus)
    on_plus = send(relay.at[0], across.at[0], z_send.at[2], z_recv.at[2], z_plus)
    on_minus = send(relay.at[1], across.at[1], z_send.at[3], z_recv.at[3], z_minus)
    meet_along_z()
    out_plus.start()
    out_minus.start()
    parity_ref[...] = scaled[0] + second_in[1] + second_in[2]
    out_plus.wait_recv()
    on_plus.start()
    out_minus.wait_recv()
    on_minus.start()

    for i in range(PARTS):
        hop(1, i).wait_recv()
        hop(2, i).start()

    on_plus.wait_recv()
    parity_ref[:, :, left] += across[0]
    on_minus.wait_recv()
    parity_ref[:, :, right] += across[1]

    for copy in (far_plus, far_minus, near_plus, near_minus, sum_plus, sum_minus):
        copy.wait_send()
    for copy in (out_plus, out_minus, on_plus, on_minus):
        copy.wait_send()
    for step in range(3):
        for i in range(PARTS):
            hop(step, i).wait_send()
    for b in short:
        plus(b).wait_send()
    for b in short:
        plus(b).wait_recv()
    for i in range(PARTS):
        hop(2, i).wait_recv()


def exchange(owners, exponents, w, m, v, g):
    shape = w.shape
    stripes, _, width = shape
    block = (3, STRIPE, width)
    halves = (2, 3, STRIPE, width // 2)
    return pl.pallas_call(
        exchange_kernel,
        out_shape=(
            pltpu.VMEM((3, *shape), F32),
            pltpu.VMEM((3, *shape), F32),
            pltpu.VMEM(block, F32),
        ),
        in_specs=[IN_HBM] * 6,
        out_specs=(IN_VMEM,) * 3,
        scratch_shapes=[
            pltpu.VMEM(shape, F32),
            pltpu.VMEM(shape, F32),
            pltpu.VMEM(shape, F32),
            pltpu.VMEM(g.shape, g.dtype),
            pltpu.SMEM(owners.shape, jnp.int32),
            pltpu.SMEM(exponents.shape, jnp.int32),
            pltpu.VMEM((XS * ZHS, *block), F32),
            pltpu.VMEM((2, *block), F32),
            pltpu.VMEM((4, *block), F32),
            pltpu.VMEM(halves, F32),
            pltpu.VMEM(halves, F32),
            pltpu.VMEM((PARTS, 3, 2, STRIPE, width // PARTS), F32),
            pltpu.VMEM((PARTS, 3, 2, STRIPE, width // PARTS), F32),
            DMA((stripes // 2 + 2, 4)),
            DMA((2,)),
            DMA((stripes // 2 + 2,)),
            DMA((stripes // 2 + 2,)),
            DMA((3, PARTS)),
            DMA((3, PARTS)),
            DMA((6,)),
            DMA((6,)),
            DMA((4,)),
            DMA((4,)),
        ],
        compiler_params=pltpu.CompilerParams(
            collective_id=0, has_side_effects=True, vmem_limit_bytes=40 << 20
        ),
        name="exchange",
    )(owners, exponents, w, m, v, g)


def finish_kernel(fresh, buddy, parity, w_out, m_out, v_out, buddy_out, parity_out, sem):
    copies = [pltpu.make_async_copy(parity, parity_out, sem.at[6, 0])]
    for h in range(CUTS):
        rows = pl.ds(h * (fresh.shape[1] // CUTS), fresh.shape[1] // CUTS)
        for a, out in enumerate((w_out, m_out, v_out)):
            copies.append(pltpu.make_async_copy(fresh.at[a, rows], out.at[rows], sem.at[a, h]))
            copies.append(
                pltpu.make_async_copy(buddy.at[a, rows], buddy_out.at[a, rows], sem.at[3 + a, h])
            )
    for copy in copies:
        copy.start()
    for copy in copies:
        copy.wait()


def finish(fresh, buddy, parity):
    one = jax.ShapeDtypeStruct(fresh.shape[1:], F32)
    return pl.pallas_call(
        finish_kernel,
        out_shape=(
            one,
            one,
            one,
            jax.ShapeDtypeStruct(buddy.shape, F32),
            jax.ShapeDtypeStruct(parity.shape, F32),
        ),
        in_specs=[IN_VMEM] * 3,
        out_specs=(IN_HBM,) * 5,
        scratch_shapes=[DMA((7, CUTS))],
        compiler_params=pltpu.CompilerParams(vmem_limit_bytes=1 << 20),
        name="finish",
    )(fresh, buddy, parity)


def shards(weight, moment1, moment2, gradient, owner_table, exponents):
    rows, width = weight.shape
    w, m, v = (a.reshape(rows // STRIPE, STRIPE, width) for a in (weight, moment1, moment2))
    held = (owner_table.T, exponents, w, m, v, gradient)
    held = (pltpu.with_memory_space_constraint(a, pltpu.HBM) for a in held)
    fresh, buddy, parity = exchange(*held)
    w, m, v, buddy, parity = finish(fresh, buddy, parity)
    buddy = jnp.transpose(buddy.reshape(3, rows, width), (1, 0, 2))
    parity = jnp.transpose(parity, (1, 0, 2))
    return (*(a.reshape(rows, width) for a in (w, m, v)), buddy, parity)


def solution(mesh):
    rows = P(("group", "domain"), None)
    blocks = P(("group", "domain"), None, None)
    return jax.shard_map(
        shards,
        mesh=mesh,
        in_specs=(rows, rows, rows, rows, P(), P()),
        out_specs=(rows, rows, rows, blocks, blocks),
        check_vma=False,
    )
```

```python
import jax
import jax.numpy as jnp
from jax import lax
from jax.experimental import pallas as pl
from jax.experimental.pallas import tpu as pltpu
from jax.sharding import PartitionSpec as P

beta_one = 0.9
beta_two = 0.95
learning_rate = 0.02
weight_decay = 0.1
epsilon = 1e-08
step_count = 100.0

MESH = pl.DeviceIdType.MESH
XS, ZS, YS, ZLS, CORES = 4, 4, 4, 2, 2
ZHS = ZS // ZLS
STRIPE = 8
PARTS = 4
CUTS = 2
F32 = jnp.float32
DMA = pltpu.SemaphoreType.DMA
IN_HBM = pl.BlockSpec(memory_space=pltpu.HBM)
IN_VMEM = pl.BlockSpec(memory_space=pltpu.VMEM)


def adamw(weight, moment1, moment2, gradient):
    grad_float = gradient.astype(F32)
    first = beta_one * moment1 + (1.0 - beta_one) * grad_float
    second = beta_two * moment2 + (1.0 - beta_two) * grad_float * grad_float
    correct_one = 1.0 - beta_one**step_count
    correct_two = 1.0 - beta_two**step_count
    update = (
        first / correct_one / (jnp.sqrt(second / correct_two) + epsilon) + weight_decay * weight
    )
    return (weight - learning_rate * update, first, second)


def coefficient(stripe, exponent):
    bits = [(jnp.right_shift(exponent, i) & 1).astype(F32) for i in range(3)]
    point = 1.0 + (2.0 * stripe.astype(F32) - 7.0) / 32.0
    square = point * point
    fourth = square * square
    power = 1.0
    for bit, factor in zip(bits, (point, square, fourth)):
        power = power * (1.0 + bit * (factor - 1.0))
    return power


def same(a, b):
    gap = a - b
    return 1 - jnp.minimum(jnp.maximum(gap, -gap), 1)


def exchange_kernel(
    owners_in, exponents_in, w_in, m_in, v_in, g_in, fresh, buddy_ref, parity_ref,
    w, m, v, g, owner_ref, exponent_ref, scaled, first_in, second_in, relay, across, hop1, hop2,
    load_sem, table_sem, plus_send, plus_recv, hop_send, hop_recv, x_send, x_recv, z_send, z_recv,
):
    group = lax.axis_index("group")
    domain = lax.axis_index("domain")
    x, zh = group % XS, group // XS
    core, zl, y = domain % CORES, (domain // CORES) % ZLS, domain // (CORES * ZLS)
    z = zh * ZLS + zl

    def device(x, y, z):
        return ((z // ZLS) * XS + x, (y * ZLS + z % ZLS) * CORES + core)

    y_plus, y_minus = device(x, (y + 1) % YS, z), device(x, (y + YS - 1) % YS, z)
    x_plus, x_minus = device((x + 1) % XS, y, z), device((x + XS - 1) % XS, y, z)
    z_plus, z_minus = device(x, y, (z + 1) % ZS), device(x, y, (z + ZS - 1) % ZS)
    stripes = w.shape[0]
    half = w.shape[2] // 2
    part = w.shape[2] // PARTS

    tables = [
        pltpu.make_async_copy(owners_in, owner_ref, table_sem.at[0]),
        pltpu.make_async_copy(exponents_in, exponent_ref, table_sem.at[1]),
    ]

    first, last = 0, stripes // 2 - 1
    blocks = [
        (first, 0, part),
        (last, 0, part),
        (first, part, half * 2 - part),
        (last, part, half * 2 - part),
    ]
    blocks += [(pair, 0, half * 2) for pair in range(first + 1, last)]

    def loads(b):
        pair, start, size = blocks[b]
        two, rows, columns = pl.ds(2 * pair, 2), pl.ds(2 * STRIPE * pair, 2 * STRIPE), pl.ds(start, size)
        ends = [(src.at[two, :, columns], dst.at[two, :, columns]) for src, dst in ((w_in, w), (m_in, m), (v_in, v))]
        ends.append((g_in.at[rows, columns], g.at[rows, columns]))
        return [pltpu.make_async_copy(*e, load_sem.at[b, i]) for i, e in enumerate(ends)]

    for b in range(len(blocks)):
        for load in loads(b):
            load.start()

    def send(source, target, send_sem, recv_sem, to):
        return pltpu.make_async_remote_copy(
            src_ref=source,
            dst_ref=target,
            send_sem=send_sem,
            recv_sem=recv_sem,
            device_id=to,
            device_id_type=MESH,
        )

    barrier = pltpu.get_barrier_semaphore()

    def greet(other):
        pl.semaphore_signal(barrier, inc=1, device_id=other, device_id_type=MESH)

    greet(y_plus)
    greet(y_minus)

    @pl.when(x < XS - 1)
    def _():
        greet(x_plus)

    @pl.when(x > 0)
    def _():
        greet(x_minus)

    x_first, z_first, z_last = 1 - jnp.minimum(x, 1), 1 - jnp.minimum(z, 1), z // (ZS - 1)

    def meet():
        pl.semaphore_wait(barrier, 4 - x_first + 1 - z_first + z_last)

        @pl.when(x == 0)
        def _():
            greet(x_minus)

        @pl.when(x == XS - 1)
        def _():
            greet(x_plus)

        greet(z_plus)
        greet(z_minus)

    def meet_the_rest():
        rest = x_first + z_first + 1 - z_last

        @pl.when(rest > 0)
        def _():
            pl.semaphore_wait(barrier, rest)

    def update(b):
        pair, start, size = blocks[b]
        columns = pl.ds(start, size)
        for load in loads(b):
            load.wait()
        gradient = g[pl.ds(2 * STRIPE * pair, 2 * STRIPE), columns].astype(F32)
        for h in range(2):
            s = 2 * pair + h
            new = adamw(
                w[s, :, columns], m[s, :, columns], v[s, :, columns],
                gradient[h * STRIPE : (h + 1) * STRIPE],
            )
            for a in range(3):
                fresh[a, s, :, columns] = new[a]

    def plus(b):
        pair, start, size = blocks[b]
        here = (slice(None), pl.ds(2 * pair, 2), slice(None), pl.ds(start, size))
        return send(fresh.at[here], buddy_ref.at[here], plus_send.at[b], plus_recv.at[b], y_plus)

    def hop(step, i):
        here = (slice(None), pl.ds(2 * last, 2), slice(None), pl.ds(i * part, part))
        source = (fresh.at[here], hop1.at[i], hop2.at[i])[step]
        target = (hop1.at[i], hop2.at[i], buddy_ref.at[here])[step]
        return send(source, target, hop_send.at[step, i], hop_recv.at[step, i], y_minus)

    short = [b for b in range(len(blocks)) if blocks[b][0] != last]

    update(0)
    meet()
    plus(0).start()
    for table in tables:
        table.start()
    update(1)
    hop(0, 0).start()
    update(2)
    plus(2).start()
    update(3)
    for i in range(1, PARTS):
        hop(0, i).start()
    for b in short[2:]:
        update(b)
        plus(b).start()

    for table in tables:
        table.wait()
    exponent = exponent_ref[group]
    meet_the_rest()

    def scale(dx, dz):
        owner = ((zh + dz) % ZHS) * XS + (x + dx) % XS
        stripe = jnp.int32(0)
        for s in range(stripes):
            stripe = stripe + s * same(owner_ref[s, domain], owner)
        stripe = jnp.minimum(stripe, stripes - 1)
        factor = coefficient(stripe, exponent)
        for a in range(3):
            scaled[dz * XS + dx, a] = fresh[a, stripe] * factor

    def along_x(i, slot, target, to):
        return send(scaled.at[slot], target, x_send.at[i], x_recv.at[i], to)

    far_plus = along_x(0, 2, first_in.at[0], x_plus)
    far_minus = along_x(1, XS + 2, first_in.at[1], x_minus)
    near_plus = along_x(2, XS + 1, second_in.at[0], x_plus)
    near_minus = along_x(3, XS - 1, second_in.at[1], x_minus)
    sum_plus = along_x(4, 1, second_in.at[2], x_plus)
    sum_minus = along_x(5, XS + XS - 1, second_in.at[3], x_minus)
    scale(2, 0)
    far_plus.start()
    scale(2, 1)
    far_minus.start()
    scale(1, 1)
    near_plus.start()
    scale(3, 0)
    near_minus.start()
    scale(1, 0)
    scale(3, 1)
    scale(0, 0)
    scale(0, 1)

    far_plus.wait_recv()
    scaled[1] += first_in[0]
    sum_plus.start()
    far_minus.wait_recv()
    scaled[XS + XS - 1] += first_in[1]
    sum_minus.start()

    for i in range(PARTS):
        hop(0, i).wait_recv()
        hop(1, i).start()

    for copy in (near_plus, near_minus, sum_plus, sum_minus):
        copy.wait_recv()
    scaled[XS] += second_in[0] + second_in[3]
    left, right = pl.ds(0, half), pl.ds(half, half)
    out_plus = send(scaled.at[XS, :, :, left], relay.at[0], z_send.at[0], z_recv.at[0], z_plus)
    out_minus = send(scaled.at[XS, :, :, right], relay.at[1], z_send.at[1], z_recv.at[1], z_minus)
    on_plus = send(relay.at[0], across.at[0], z_send.at[2], z_recv.at[2], z_plus)
    on_minus = send(relay.at[1], across.at[1], z_send.at[3], z_recv.at[3], z_minus)
    out_plus.start()
    out_minus.start()
    parity_ref[...] = scaled[0] + second_in[1] + second_in[2]
    out_plus.wait_recv()
    on_plus.start()
    out_minus.wait_recv()
    on_minus.start()

    for i in range(PARTS):
        hop(1, i).wait_recv()
        hop(2, i).start()

    on_plus.wait_recv()
    parity_ref[:, :, left] += across[0]
    on_minus.wait_recv()
    parity_ref[:, :, right] += across[1]

    for copy in (far_plus, far_minus, near_plus, near_minus, sum_plus, sum_minus):
        copy.wait_send()
    for copy in (out_plus, out_minus, on_plus, on_minus):
        copy.wait_send()
    for step in range(3):
        for i in range(PARTS):
            hop(step, i).wait_send()
    for b in short:
        plus(b).wait_send()
    for b in short:
        plus(b).wait_recv()
    for i in range(PARTS):
        hop(2, i).wait_recv()


def exchange(owners, exponents, w, m, v, g):
    shape = w.shape
    stripes, _, width = shape
    block = (3, STRIPE, width)
    halves = (2, 3, STRIPE, width // 2)
    return pl.pallas_call(
        exchange_kernel,
        out_shape=(
            pltpu.VMEM((3, *shape), F32),
            pltpu.VMEM((3, *shape), F32),
            pltpu.VMEM(block, F32),
        ),
        in_specs=[IN_HBM] * 6,
        out_specs=(IN_VMEM,) * 3,
        scratch_shapes=[
            pltpu.VMEM(shape, F32),
            pltpu.VMEM(shape, F32),
            pltpu.VMEM(shape, F32),
            pltpu.VMEM(g.shape, g.dtype),
            pltpu.SMEM(owners.shape, jnp.int32),
            pltpu.SMEM(exponents.shape, jnp.int32),
            pltpu.VMEM((XS * ZHS, *block), F32),
            pltpu.VMEM((2, *block), F32),
            pltpu.VMEM((4, *block), F32),
            pltpu.VMEM(halves, F32),
            pltpu.VMEM(halves, F32),
            pltpu.VMEM((PARTS, 3, 2, STRIPE, width // PARTS), F32),
            pltpu.VMEM((PARTS, 3, 2, STRIPE, width // PARTS), F32),
            DMA((stripes // 2 + 2, 4)),
            DMA((2,)),
            DMA((stripes // 2 + 2,)),
            DMA((stripes // 2 + 2,)),
            DMA((3, PARTS)),
            DMA((3, PARTS)),
            DMA((6,)),
            DMA((6,)),
            DMA((4,)),
            DMA((4,)),
        ],
        compiler_params=pltpu.CompilerParams(
            collective_id=0, has_side_effects=True, vmem_limit_bytes=40 << 20
        ),
        name="exchange",
    )(owners, exponents, w, m, v, g)


def finish_kernel(fresh, buddy, parity, w_out, m_out, v_out, buddy_out, parity_out, sem):
    copies = [pltpu.make_async_copy(parity, parity_out, sem.at[6, 0])]
    for h in range(CUTS):
        rows = pl.ds(h * (fresh.shape[1] // CUTS), fresh.shape[1] // CUTS)
        for a, out in enumerate((w_out, m_out, v_out)):
            copies.append(pltpu.make_async_copy(fresh.at[a, rows], out.at[rows], sem.at[a, h]))
            copies.append(
                pltpu.make_async_copy(buddy.at[a, rows], buddy_out.at[a, rows], sem.at[3 + a, h])
            )
    for copy in copies:
        copy.start()
    for copy in copies:
        copy.wait()


def finish(fresh, buddy, parity):
    one = jax.ShapeDtypeStruct(fresh.shape[1:], F32)
    return pl.pallas_call(
        finish_kernel,
        out_shape=(
            one,
            one,
            one,
            jax.ShapeDtypeStruct(buddy.shape, F32),
            jax.ShapeDtypeStruct(parity.shape, F32),
        ),
        in_specs=[IN_VMEM] * 3,
        out_specs=(IN_HBM,) * 5,
        scratch_shapes=[DMA((7, CUTS))],
        compiler_params=pltpu.CompilerParams(vmem_limit_bytes=1 << 20),
        name="finish",
    )(fresh, buddy, parity)


def shards(weight, moment1, moment2, gradient, owner_table, exponents):
    rows, width = weight.shape
    w, m, v = (a.reshape(rows // STRIPE, STRIPE, width) for a in (weight, moment1, moment2))
    held = (owner_table.T, exponents, w, m, v, gradient)
    held = (pltpu.with_memory_space_constraint(a, pltpu.HBM) for a in held)
    fresh, buddy, parity = exchange(*held)
    w, m, v, buddy, parity = finish(fresh, buddy, parity)
    buddy = jnp.transpose(buddy.reshape(3, rows, width), (1, 0, 2))
    parity = jnp.transpose(parity, (1, 0, 2))
    return (*(a.reshape(rows, width) for a in (w, m, v)), buddy, parity)


def solution(mesh):
    rows = P(("group", "domain"), None)
    blocks = P(("group", "domain"), None, None)
    return jax.shard_map(
        shards,
        mesh=mesh,
        in_specs=(rows, rows, rows, rows, P(), P()),
        out_specs=(rows, rows, rows, blocks, blocks),
        check_vma=False,
    )
```

```python
import jax
import jax.numpy as jnp
from jax import lax
from jax.experimental import pallas as pl
from jax.experimental.pallas import tpu as pltpu
from jax.sharding import PartitionSpec as P

beta_one = 0.9
beta_two = 0.95
learning_rate = 0.02
weight_decay = 0.1
epsilon = 1e-08
step_count = 100.0

MESH = pl.DeviceIdType.MESH
XS, ZS, YS, ZLS, CORES = 4, 4, 4, 2, 2
ZHS = ZS // ZLS
STRIPE = 8
PARTS = (512, 2048, 2176, 2304)
EXTRA = 128
CUTS = 2
F32 = jnp.float32
DMA = pltpu.SemaphoreType.DMA
IN_HBM = pl.BlockSpec(memory_space=pltpu.HBM)
IN_VMEM = pl.BlockSpec(memory_space=pltpu.VMEM)


def adamw(weight, moment1, moment2, gradient):
    grad_float = gradient.astype(F32)
    first = beta_one * moment1 + (1.0 - beta_one) * grad_float
    second = beta_two * moment2 + (1.0 - beta_two) * grad_float * grad_float
    correct_one = 1.0 - beta_one**step_count
    correct_two = 1.0 - beta_two**step_count
    scaled_second = second * (1.0 / correct_two)
    spread = scaled_second * lax.rsqrt(scaled_second) + epsilon
    step = first * (learning_rate / correct_one) / spread
    return (weight * (1.0 - learning_rate * weight_decay) - step, first, second)


def coefficient(stripe, exponent):
    bits = [(jnp.right_shift(exponent, i) & 1).astype(F32) for i in range(3)]
    point = 1.0 + (2.0 * stripe.astype(F32) - 7.0) / 32.0
    square = point * point
    fourth = square * square
    power = 1.0
    for bit, factor in zip(bits, (point, square, fourth)):
        power = power * (1.0 + bit * (factor - 1.0))
    return power


def same(a, b):
    gap = a - b
    return 1 - jnp.minimum(jnp.maximum(gap, -gap), 1)


def exchange_kernel(
    owners_in, exponents_in, w_in, m_in, v_in, g_in, fresh, buddy_ref, parity_ref,
    w, m, v, g, owner_ref, exponent_ref, scaled, first_in, second_in, relay, across, hop1, hop2, extra1, extra2,
    load_sem, table_sem, plus_send, plus_recv, hop_send, hop_recv, x_send, x_recv, z_send, z_recv, ring_sem,
):
    group = lax.axis_index("group")
    domain = lax.axis_index("domain")
    x, zh = group % XS, group // XS
    core, zl, y = domain % CORES, (domain // CORES) % ZLS, domain // (CORES * ZLS)
    z = zh * ZLS + zl

    def device(x, y, z):
        return ((z // ZLS) * XS + x, (y * ZLS + z % ZLS) * CORES + core)

    y_plus, y_minus = device(x, (y + 1) % YS, z), device(x, (y + YS - 1) % YS, z)
    x_plus, x_minus = device((x + 1) % XS, y, z), device((x + XS - 1) % XS, y, z)
    z_plus, z_minus = device(x, y, (z + 1) % ZS), device(x, y, (z + ZS - 1) % ZS)
    stripes = w.shape[0]
    half = w.shape[2] // 2
    width = w.shape[2]
    short_width = width - EXTRA

    tables = [
        pltpu.make_async_copy(owners_in, owner_ref, table_sem.at[0]),
        pltpu.make_async_copy(exponents_in, exponent_ref, table_sem.at[1]),
    ]

    first, last = 0, stripes // 2 - 1
    blocks = [
        (first, 0, PARTS[0]),
        (last, 0, PARTS[0]),
        (first, PARTS[0], width - PARTS[0]),
        (last, PARTS[0], width - PARTS[0]),
    ]
    blocks += [(pair, 0, width) for pair in range(first + 1, last)]

    def loads(b):
        pair, start, size = blocks[b]
        two, rows, columns = pl.ds(2 * pair, 2), pl.ds(2 * STRIPE * pair, 2 * STRIPE), pl.ds(start, size)
        ends = [(src.at[two, :, columns], dst.at[two, :, columns]) for src, dst in ((w_in, w), (m_in, m), (v_in, v))]
        ends.append((g_in.at[rows, columns], g.at[rows, columns]))
        return [pltpu.make_async_copy(*e, load_sem.at[b, i]) for i, e in enumerate(ends)]

    for b in range(len(blocks)):
        for load in loads(b):
            load.start()

    def send(source, target, send_sem, recv_sem, to):
        return pltpu.make_async_remote_copy(
            src_ref=source,
            dst_ref=target,
            send_sem=send_sem,
            recv_sem=recv_sem,
            device_id=to,
            device_id_type=MESH,
        )

    barrier = pltpu.get_barrier_semaphore()

    def greet(*others, semaphore=barrier):
        for other in others:
            pl.semaphore_signal(semaphore, inc=1, device_id=other, device_id_type=MESH)

    greet(y_plus, y_minus)

    @pl.when(y == 0)
    def _():
        greet(x_plus, x_minus)

        @pl.when(z < ZS - 1)
        def _():
            greet(z_plus)

        @pl.when(z > 0)
        def _():
            greet(z_minus)

    def meet():
        @pl.when(y > 0)
        def _():
            pl.semaphore_wait(barrier, 2)

        @pl.when((y == 0) & (z == 0))
        def _():
            pl.semaphore_wait(barrier, 5)
            greet(z_minus)

        @pl.when((y == 0) & (z > 0))
        def _():
            pl.semaphore_wait(barrier, 6)

        @pl.when((y == 0) & (z == ZS - 1))
        def _():
            greet(z_plus)

        @pl.when(y == 1)
        def _():
            greet(y_minus, semaphore=ring_sem.at[0])

    def meet_the_rest():
        @pl.when((y == 0) & (z == 0))
        def _():
            pl.semaphore_wait(barrier, 1)

        @pl.when(y == 0)
        def _():
            pl.semaphore_wait(ring_sem.at[0], 1)
            greet(x_plus, x_minus, z_plus, z_minus, semaphore=ring_sem.at[1])
            pl.semaphore_wait(ring_sem.at[1], 4)
            greet(y_plus, y_minus, semaphore=ring_sem.at[2])

        @pl.when(y > 0)
        def _():
            pl.semaphore_wait(ring_sem.at[2], 1)

        @pl.when(y == 1)
        def _():
            greet(y_plus, semaphore=ring_sem.at[2])

    def update(b):
        pair, start, size = blocks[b]
        columns = pl.ds(start, size)
        for load in loads(b):
            load.wait()
        gradient = g[pl.ds(2 * STRIPE * pair, 2 * STRIPE), columns].astype(F32)
        for h in range(2):
            s = 2 * pair + h
            new = adamw(
                w[s, :, columns], m[s, :, columns], v[s, :, columns],
                gradient[h * STRIPE : (h + 1) * STRIPE],
            )
            for a in range(3):
                fresh[a, s, :, columns] = new[a]

    def plus(b):
        pair, start, size = blocks[b]
        if pair == last - 1:
            size = short_width - start
        here = (slice(None), pl.ds(2 * pair, 2), slice(None), pl.ds(start, size))
        return send(fresh.at[here], buddy_ref.at[here], plus_send.at[b], plus_recv.at[b], y_plus)

    def hop(step, i):
        start, size = sum(PARTS[:i]), PARTS[i]
        here = (slice(None), pl.ds(2 * last, 2), slice(None), pl.ds(start, size))
        held = (i, slice(None), slice(None), slice(None), pl.ds(0, size))
        source = (fresh.at[here], hop1.at[held], hop2.at[held])[step]
        target = (hop1.at[held], hop2.at[held], buddy_ref.at[here])[step]
        return send(source, target, hop_send.at[step, i], hop_recv.at[step, i], y_minus)

    left_over = (slice(None), pl.ds(2 * last - 2, 4), slice(None), pl.ds(short_width, EXTRA))

    def plus_extra():
        here = (fresh.at[left_over], buddy_ref.at[left_over])
        return send(*here, plus_send.at[1], plus_recv.at[1], y_plus)

    def hop_extra(step):
        source = (fresh.at[left_over], extra1, extra2)[step]
        target = (extra1, extra2, buddy_ref.at[left_over])[step]
        return send(source, target, hop_send.at[step, len(PARTS)], hop_recv.at[step, len(PARTS)], y_minus)

    def by_start(behind, act_long, act_short):
        goes_long = ((y + behind + 1) % YS) // 2 == 0
        if act_long is not None:
            pl.when(goes_long)(act_long)
        if act_short is not None:
            pl.when(jnp.logical_not(goes_long))(act_short)

    def pass_on(step):
        for i in range(len(PARTS)):
            hop(step, i).wait_recv()
            hop(step + 1, i).start()

        def extra():
            hop_extra(step).wait_recv()
            hop_extra(step + 1).start()

        by_start(step + 1, extra, None)

    short = [b for b in range(len(blocks)) if blocks[b][0] != last]

    update(0)
    meet()
    plus(0).start()
    for table in tables:
        table.start()
    update(1)
    hop(0, 0).start()
    update(2)
    plus(2).start()
    update(3)
    for i in range(1, len(PARTS)):
        hop(0, i).start()
    for b in short[2:]:
        update(b)
        plus(b).start()
    by_start(0, lambda: hop_extra(0).start(), lambda: plus_extra().start())

    for table in tables:
        table.wait()
    exponent = exponent_ref[group]
    meet_the_rest()

    def scale(dx, dz):
        owner = ((zh + dz) % ZHS) * XS + (x + dx) % XS
        stripe = jnp.int32(0)
        for s in range(stripes):
            stripe = stripe + s * same(owner_ref[s, domain], owner)
        stripe = jnp.minimum(stripe, stripes - 1)
        factor = coefficient(stripe, exponent)
        for a in range(3):
            scaled[dz * XS + dx, a] = fresh[a, stripe] * factor

    def along_x(i, slot, target, to):
        return send(scaled.at[slot], target, x_send.at[i], x_recv.at[i], to)

    far_plus = along_x(0, 2, first_in.at[0], x_plus)
    far_minus = along_x(1, XS + 2, first_in.at[1], x_minus)
    near_plus = along_x(2, XS + 1, second_in.at[0], x_plus)
    near_minus = along_x(3, XS - 1, second_in.at[1], x_minus)
    sum_plus = along_x(4, 1, second_in.at[2], x_plus)
    sum_minus = along_x(5, XS + XS - 1, second_in.at[3], x_minus)
    scale(2, 0)
    far_plus.start()
    scale(2, 1)
    far_minus.start()
    scale(1, 1)
    near_plus.start()
    scale(3, 0)
    near_minus.start()
    scale(1, 0)
    scale(3, 1)
    scale(0, 0)
    scale(0, 1)

    far_plus.wait_recv()
    scaled[1] += first_in[0]
    sum_plus.start()
    far_minus.wait_recv()
    scaled[XS + XS - 1] += first_in[1]
    sum_minus.start()

    pass_on(0)

    for copy in (near_plus, near_minus, sum_plus, sum_minus):
        copy.wait_recv()
    scaled[XS] += second_in[0] + second_in[3]
    left, right = pl.ds(0, half), pl.ds(half, half)
    out_plus = send(scaled.at[XS, :, :, left], relay.at[0], z_send.at[0], z_recv.at[0], z_plus)
    out_minus = send(scaled.at[XS, :, :, right], relay.at[1], z_send.at[1], z_recv.at[1], z_minus)
    on_plus = send(relay.at[0], across.at[0], z_send.at[2], z_recv.at[2], z_plus)
    on_minus = send(relay.at[1], across.at[1], z_send.at[3], z_recv.at[3], z_minus)
    out_plus.start()
    out_minus.start()
    parity_ref[...] = scaled[0] + second_in[1] + second_in[2]

    pass_on(1)

    out_plus.wait_recv()
    on_plus.start()
    out_minus.wait_recv()
    on_minus.start()
    on_plus.wait_recv()
    parity_ref[:, :, left] += across[0]
    on_minus.wait_recv()
    parity_ref[:, :, right] += across[1]

    for copy in (far_plus, far_minus, near_plus, near_minus, sum_plus, sum_minus):
        copy.wait_send()
    for copy in (out_plus, out_minus, on_plus, on_minus):
        copy.wait_send()
    for step in range(3):
        for i in range(len(PARTS)):
            hop(step, i).wait_send()
        by_start(step, lambda: hop_extra(step).wait_send(), None)
    by_start(0, None, lambda: plus_extra().wait_send())
    for b in short:
        plus(b).wait_send()
    by_start(YS - 1, None, lambda: plus_extra().wait_recv())
    for b in short:
        plus(b).wait_recv()
    for i in range(len(PARTS)):
        hop(2, i).wait_recv()
    by_start(YS - 1, lambda: hop_extra(2).wait_recv(), None)


def exchange(owners, exponents, w, m, v, g):
    shape = w.shape
    stripes, _, width = shape
    block = (3, STRIPE, width)
    halves = (2, 3, STRIPE, width // 2)
    return pl.pallas_call(
        exchange_kernel,
        out_shape=(
            pltpu.VMEM((3, *shape), F32),
            pltpu.VMEM((3, *shape), F32),
            pltpu.VMEM(block, F32),
        ),
        in_specs=[IN_HBM] * 6,
        out_specs=(IN_VMEM,) * 3,
        scratch_shapes=[
            pltpu.VMEM(shape, F32),
            pltpu.VMEM(shape, F32),
            pltpu.VMEM(shape, F32),
            pltpu.VMEM(g.shape, g.dtype),
            pltpu.SMEM(owners.shape, jnp.int32),
            pltpu.SMEM(exponents.shape, jnp.int32),
            pltpu.VMEM((XS * ZHS, *block), F32),
            pltpu.VMEM((2, *block), F32),
            pltpu.VMEM((4, *block), F32),
            pltpu.VMEM(halves, F32),
            pltpu.VMEM(halves, F32),
            pltpu.VMEM((len(PARTS), 3, 2, STRIPE, max(PARTS)), F32),
            pltpu.VMEM((len(PARTS), 3, 2, STRIPE, max(PARTS)), F32),
            pltpu.VMEM((3, 4, STRIPE, EXTRA), F32),
            pltpu.VMEM((3, 4, STRIPE, EXTRA), F32),
            DMA((stripes // 2 + 2, 4)),
            DMA((2,)),
            DMA((stripes // 2 + 2,)),
            DMA((stripes // 2 + 2,)),
            DMA((3, len(PARTS) + 1)),
            DMA((3, len(PARTS) + 1)),
            DMA((6,)),
            DMA((6,)),
            DMA((4,)),
            DMA((4,)),
            pltpu.SemaphoreType.REGULAR((3,)),
        ],
        compiler_params=pltpu.CompilerParams(
            collective_id=0, has_side_effects=True, vmem_limit_bytes=40 << 20
        ),
        name="exchange",
    )(owners, exponents, w, m, v, g)


def finish_kernel(fresh, buddy, parity, w_out, m_out, v_out, buddy_out, parity_out, sem):
    copies = [pltpu.make_async_copy(parity, parity_out, sem.at[6, 0])]
    for h in range(CUTS):
        rows = pl.ds(h * (fresh.shape[1] // CUTS), fresh.shape[1] // CUTS)
        for a, out in enumerate((w_out, m_out, v_out)):
            copies.append(pltpu.make_async_copy(fresh.at[a, rows], out.at[rows], sem.at[a, h]))
            copies.append(
                pltpu.make_async_copy(buddy.at[a, rows], buddy_out.at[a, rows], sem.at[3 + a, h])
            )
    for copy in copies:
        copy.start()
    for copy in copies:
        copy.wait()


def finish(fresh, buddy, parity):
    one = jax.ShapeDtypeStruct(fresh.shape[1:], F32)
    return pl.pallas_call(
        finish_kernel,
        out_shape=(
            one,
            one,
            one,
            jax.ShapeDtypeStruct(buddy.shape, F32),
            jax.ShapeDtypeStruct(parity.shape, F32),
        ),
        in_specs=[IN_VMEM] * 3,
        out_specs=(IN_HBM,) * 5,
        scratch_shapes=[DMA((7, CUTS))],
        compiler_params=pltpu.CompilerParams(vmem_limit_bytes=1 << 20),
        name="finish",
    )(fresh, buddy, parity)


def shards(weight, moment1, moment2, gradient, owner_table, exponents):
    rows, width = weight.shape
    w, m, v = (a.reshape(rows // STRIPE, STRIPE, width) for a in (weight, moment1, moment2))
    held = (owner_table.T, exponents, w, m, v, gradient)
    held = (pltpu.with_memory_space_constraint(a, pltpu.HBM) for a in held)
    fresh, buddy, parity = exchange(*held)
    w, m, v, buddy, parity = finish(fresh, buddy, parity)
    buddy = jnp.transpose(buddy.reshape(3, rows, width), (1, 0, 2))
    parity = jnp.transpose(parity, (1, 0, 2))
    return (*(a.reshape(rows, width) for a in (w, m, v)), buddy, parity)


def solution(mesh):
    rows = P(("group", "domain"), None)
    blocks = P(("group", "domain"), None, None)
    return jax.shard_map(
        shards,
        mesh=mesh,
        in_specs=(rows, rows, rows, rows, P(), P()),
        out_specs=(rows, rows, rows, blocks, blocks),
        check_vma=False,
    )
```

```python
import jax
import jax.numpy as jnp
from jax import lax
from jax.experimental import pallas as pl
from jax.experimental.pallas import tpu as pltpu
from jax.sharding import PartitionSpec as P

beta_one = 0.9
beta_two = 0.95
learning_rate = 0.02
weight_decay = 0.1
epsilon = 1e-08
step_count = 100.0

MESH = pl.DeviceIdType.MESH
XS, ZS, YS, ZLS, CORES = 4, 4, 4, 2, 2
ZHS = ZS // ZLS
STRIPE = 8
LONG = (
    (((0, 512), (512, 1536), (2048, 1536)), ((3584, 1152), (4736, 1152), (5888, 1280))),
    (((0, 512), (512, 2304), (2816, 2304)), ((5120, 1024), (6144, 1024))),
)
SHORT = (
    (((0, 0, 512), (0, 512, 6656), (1, 0, 3584)), ((1, 3584, 3584), (2, 0, 7168))),
    (((0, 0, 512), (0, 512, 6656), (1, 0, 7168), (2, 0, 1024)), ((2, 1024, 6144),)),
)
F32 = jnp.float32
DMA = pltpu.SemaphoreType.DMA
IN_HBM = pl.BlockSpec(memory_space=pltpu.HBM)
IN_VMEM = pl.BlockSpec(memory_space=pltpu.VMEM)


def adamw(weight, moment1, moment2, gradient):
    grad_float = gradient.astype(F32)
    first = beta_one * moment1 + (1.0 - beta_one) * grad_float
    second = beta_two * moment2 + (1.0 - beta_two) * grad_float * grad_float
    correct_one = 1.0 - beta_one**step_count
    correct_two = 1.0 - beta_two**step_count
    scaled_second = second * (1.0 / correct_two)
    spread = scaled_second * lax.rsqrt(scaled_second) + epsilon
    step = first * (learning_rate / correct_one) / spread
    return (weight * (1.0 - learning_rate * weight_decay) - step, first, second)


def coefficient(stripe, exponent):
    bits = [(jnp.right_shift(exponent, i) & 1).astype(F32) for i in range(3)]
    point = 1.0 + (2.0 * stripe.astype(F32) - 7.0) / 32.0
    square = point * point
    fourth = square * square
    power = 1.0
    for bit, factor in zip(bits, (point, square, fourth)):
        power = power * (1.0 + bit * (factor - 1.0))
    return power


def same(a, b):
    gap = a - b
    return 1 - jnp.minimum(jnp.maximum(gap, -gap), 1)


def loading_kernel(
    owners_in, exponents_in, w_in, m_in, v_in, g_in, fresh, buddy_ref, part_ref, cross_ref,
    w, m, v, g, load_sem, *rest,
):
    last, width = w.shape[0] // 2 - 1, w.shape[2]
    cut = LONG[0][0][0][1]
    blocks = [(0, 0, cut), (last, 0, cut), (0, cut, width - cut), (last, cut, width - cut)]
    blocks += [(pair, 0, width) for pair in range(1, last)]

    def loads(b):
        pair, start, size = blocks[b]
        two, rows, columns = pl.ds(2 * pair, 2), pl.ds(2 * STRIPE * pair, 2 * STRIPE), pl.ds(start, size)
        ends = [(src.at[two, :, columns], dst.at[two, :, columns]) for src, dst in ((w_in, w), (m_in, m), (v_in, v))]
        ends.append((g_in.at[rows, columns], g.at[rows, columns]))
        return [pltpu.make_async_copy(*e, load_sem.at[b, i]) for i, e in enumerate(ends)]

    def update(b):
        pair, start, size = blocks[b]
        columns = pl.ds(start, size)
        for load in loads(b):
            load.wait()
        gradient = g[pl.ds(2 * STRIPE * pair, 2 * STRIPE), columns].astype(F32)
        for h in range(2):
            s = 2 * pair + h
            new = adamw(
                w[s, :, columns], m[s, :, columns], v[s, :, columns],
                gradient[h * STRIPE : (h + 1) * STRIPE],
            )
            for a in range(3):
                fresh[a, s, :, columns] = new[a]

    def start_loads():
        for b in range(len(blocks)):
            for load in loads(b):
                load.start()

    arrays = (fresh, buddy_ref, part_ref, cross_ref)
    exchange_kernel(0, arrays, rest, (start_loads, update, owners_in, exponents_in))


def second_kernel(fresh, after, part_ref, cross_ref, buddy_ref, parity_ref, *rest):
    exchange_kernel(1, (fresh, buddy_ref, part_ref, cross_ref), rest, parity_ref)


def exchange_kernel(phase, arrays, scratch, more):
    fresh, buddy_ref, part_ref, cross_ref = arrays
    hop1, hop2, plus_send, plus_recv, hop_send, hop_recv, ring_sem = scratch[:7]
    if phase == 0:
        start_loads, update, owners_in, exponents_in = more
        owner_ref, exponent_ref, scaled, first_in, second_in, table_sem, x_send, x_recv = scratch[7:]
    else:
        parity_ref = more
        relay, across, z_send, z_recv = scratch[7:]
    group = lax.axis_index("group")
    domain = lax.axis_index("domain")
    x, zh = group % XS, group // XS
    core, zl, y = domain % CORES, (domain // CORES) % ZLS, domain // (CORES * ZLS)
    z = zh * ZLS + zl

    def device(x, y, z):
        return ((z // ZLS) * XS + x, (y * ZLS + z % ZLS) * CORES + core)

    y_plus, y_minus = device(x, (y + 1) % YS, z), device(x, (y + YS - 1) % YS, z)
    x_plus, x_minus = device((x + 1) % XS, y, z), device((x + XS - 1) % XS, y, z)
    z_plus, z_minus = device(x, y, (z + 1) % ZS), device(x, y, (z + ZS - 1) % ZS)
    stripes = fresh.shape[1]
    half = fresh.shape[3] // 2
    last = stripes // 2 - 1

    if phase == 0:
        start_loads()

    def send(source, target, send_sem, recv_sem, to):
        return pltpu.make_async_remote_copy(
            src_ref=source,
            dst_ref=target,
            send_sem=send_sem,
            recv_sem=recv_sem,
            device_id=to,
            device_id_type=MESH,
        )

    barrier = pltpu.get_barrier_semaphore()

    def greet(*others, semaphore=barrier):
        for other in others:
            pl.semaphore_signal(semaphore, inc=1, device_id=other, device_id_type=MESH)

    greet(y_plus, y_minus)

    corner = y == 0

    @pl.when(corner)
    def _():
        greet(x_plus, x_minus)

        @pl.when(z < ZS - 1)
        def _():
            greet(z_plus)

        @pl.when(z > 0)
        def _():
            greet(z_minus)

    if phase == 0:
        update(0)

    @pl.when(jnp.logical_not(corner))
    def _():
        pl.semaphore_wait(barrier, 2)

    @pl.when(corner & (z == 0))
    def _():
        pl.semaphore_wait(barrier, 5)
        greet(z_minus)

    @pl.when(corner & (z > 0))
    def _():
        pl.semaphore_wait(barrier, 6)

    @pl.when(corner & (z == ZS - 1))
    def _():
        greet(z_plus)

    @pl.when(y == 1)
    def _():
        greet(y_minus, semaphore=ring_sem.at[0])

    def meet_the_rest():
        @pl.when((y == 0) & (z == 0))
        def _():
            pl.semaphore_wait(barrier, 1)

        @pl.when(y == 0)
        def _():
            pl.semaphore_wait(ring_sem.at[0], 1)
            greet(x_plus, x_minus, z_plus, z_minus, semaphore=ring_sem.at[1])
            pl.semaphore_wait(ring_sem.at[1], 4)
            greet(y_plus, y_minus, semaphore=ring_sem.at[2])

        @pl.when(y > 0)
        def _():
            pl.semaphore_wait(ring_sem.at[2], 1)

        @pl.when(y == 1)
        def _():
            greet(y_plus, semaphore=ring_sem.at[2])

    def short(c):
        copies = []
        for i, (pair, start, size) in enumerate(SHORT[c][phase]):
            here = (slice(None), pl.ds(2 * pair, 2), slice(None), pl.ds(start, size))
            copies.append(send(fresh.at[here], buddy_ref.at[here], plus_send.at[i], plus_recv.at[i], y_plus))
        return copies

    def hops(c, step):
        copies = []
        for i, (start, size) in enumerate(LONG[c][phase]):
            here = (slice(None), pl.ds(2 * last, 2), slice(None), pl.ds(start, size))
            held = (i, slice(None), slice(None), slice(None), pl.ds(0, size))
            source = (fresh.at[here], hop1.at[held], hop2.at[held])[step]
            target = (hop1.at[held], hop2.at[held], buddy_ref.at[here])[step]
            copies.append(send(source, target, hop_send.at[step, i], hop_recv.at[step, i], y_minus))
        return copies

    def by_core(act):
        for c in range(CORES):
            pl.when(core == c)(lambda c=c: act(c))

    def start_all(copies):
        for copy in copies:
            copy.start()

    def pass_on(c, step, chunks=slice(None)):
        for arrived, on in list(zip(hops(c, step), hops(c, step + 1)))[chunks]:
            arrived.wait_recv()
            on.start()

    def end(c):
        for step in range(3):
            for copy in hops(c, step):
                copy.wait_send()
        for copy in short(c):
            copy.wait()
        for copy in hops(c, 2):
            copy.wait_recv()

    if phase == 1:
        left, right = pl.ds(0, half), pl.ds(half, half)
        out_plus = send(cross_ref.at[:, :, left], relay.at[0], z_send.at[0], z_recv.at[0], z_plus)
        out_minus = send(cross_ref.at[:, :, right], relay.at[1], z_send.at[1], z_recv.at[1], z_minus)
        on_plus = send(relay.at[0], across.at[0], z_send.at[2], z_recv.at[2], z_plus)
        on_minus = send(relay.at[1], across.at[1], z_send.at[3], z_recv.at[3], z_minus)

        def totals():
            out_plus.wait_recv()
            on_plus.start()
            out_minus.wait_recv()
            on_minus.start()
            on_plus.wait_recv()
            parity_ref[:, :, left] = part_ref[:, :, left] + across[0]
            on_minus.wait_recv()
            parity_ref[:, :, right] = part_ref[:, :, right] + across[1]
            for copy in (out_plus, out_minus, on_plus, on_minus):
                copy.wait_send()

        def all_of(c):
            start_all(hops(c, 0) + short(c))
            meet_the_rest()
            out_plus.start()
            out_minus.start()
            pass_on(c, 0)
            pass_on(c, 1)
            totals()
            end(c)

        by_core(all_of)
        return

    tables = [
        pltpu.make_async_copy(owners_in, owner_ref, table_sem.at[0]),
        pltpu.make_async_copy(exponents_in, exponent_ref, table_sem.at[1]),
    ]
    by_core(lambda c: short(c)[0].start())
    start_all(tables)
    update(1)
    by_core(lambda c: hops(c, 0)[0].start())
    update(2)
    by_core(lambda c: short(c)[1].start())
    update(3)
    by_core(lambda c: start_all(hops(c, 0)[1:]))
    update(4)
    by_core(lambda c: short(c)[2].start())
    update(5)
    by_core(lambda c: start_all(short(c)[3:]))
    for table in tables:
        table.wait()
    meet_the_rest()

    def scale(dx, dz):
        owner = ((zh + dz) % ZHS) * XS + (x + dx) % XS
        stripe = jnp.int32(0)
        for s in range(stripes):
            stripe = stripe + s * same(owner_ref[s, domain], owner)
        stripe = jnp.minimum(stripe, stripes - 1)
        factor = coefficient(stripe, exponent_ref[group])
        for a in range(3):
            scaled[dz * XS + dx, a] = fresh[a, stripe] * factor

    def along_x(i, slot, target, to):
        return send(scaled.at[slot], target, x_send.at[i], x_recv.at[i], to)

    far_plus = along_x(0, 2, first_in.at[0], x_plus)
    far_minus = along_x(1, XS + 2, first_in.at[1], x_minus)
    near_plus = along_x(2, XS + 1, second_in.at[0], x_plus)
    near_minus = along_x(3, XS - 1, second_in.at[1], x_minus)
    sum_plus = along_x(4, 1, second_in.at[2], x_plus)
    sum_minus = along_x(5, XS + XS - 1, second_in.at[3], x_minus)
    def terms():
        scale(2, 0)
        far_plus.start()
        scale(2, 1)
        far_minus.start()
        scale(1, 1)
        near_plus.start()
        scale(3, 0)
        near_minus.start()
        scale(1, 0)
        scale(3, 1)
        scale(0, 0)
        scale(0, 1)

    def first_sums():
        far_plus.wait_recv()
        scaled[1] += first_in[0]
        sum_plus.start()
        far_minus.wait_recv()
        scaled[XS + XS - 1] += first_in[1]
        sum_minus.start()

    def sums():
        for copy in (near_plus, near_minus, sum_plus, sum_minus):
            copy.wait_recv()
        cross_ref[...] = scaled[XS] + second_in[0] + second_in[3]
        part_ref[...] = scaled[0] + second_in[1] + second_in[2]
        for copy in (far_plus, far_minus, near_plus, near_minus, sum_plus, sum_minus):
            copy.wait_send()

    @pl.when(core == 0)
    def _():
        terms()
        pass_on(0, 0)
        first_sums()
        pass_on(0, 1)
        sums()
        end(0)

    @pl.when(core == 1)
    def _():
        pass_on(1, 0)
        terms()
        pass_on(1, 1, slice(0, 2))
        first_sums()
        pass_on(1, 1, slice(2, None))
        sums()
        end(1)


def exchange(phase, shape, *arrays):
    stripes, _, width = shape
    block = (3, STRIPE, width)
    halves = (2, 3, STRIPE, width // 2)
    most_long = max(len(core[phase]) for core in LONG)
    most_short = max(len(core[phase]) for core in SHORT)
    held = (most_long, 3, 2, STRIPE, max(size for core in LONG for _, size in core[phase]))
    whole = pltpu.VMEM((3, *shape), F32)
    scratch = [pltpu.VMEM(held, F32)] * 2 + [DMA((most_short,))] * 2 + [DMA((3, most_long))] * 2
    scratch += [pltpu.SemaphoreType.REGULAR((3,))]
    if phase == 0:
        gradient = arrays[5]
        loaded = [pltpu.VMEM(shape, F32)] * 3 + [pltpu.VMEM(gradient.shape, gradient.dtype)]
        scratch = [*loaded, DMA((stripes // 2 + 2, 4)), *scratch]
        scratch += [
            pltpu.SMEM(arrays[0].shape, jnp.int32),
            pltpu.SMEM(arrays[1].shape, jnp.int32),
            pltpu.VMEM((XS * ZHS, *block), F32),
            pltpu.VMEM((2, *block), F32),
            pltpu.VMEM((4, *block), F32),
            DMA((2,)),
            DMA((6,)),
            DMA((6,)),
        ]
    else:
        scratch += [pltpu.VMEM(halves, F32)] * 2 + [DMA((4,))] * 2
    part = pltpu.VMEM(block, F32)
    return pl.pallas_call(
        (loading_kernel, second_kernel)[phase],
        out_shape=((whole, whole, part, part), (whole, part))[phase],
        in_specs=([IN_HBM] * 6, [IN_VMEM] * 4)[phase],
        out_specs=(IN_VMEM,) * (4, 2)[phase],
        scratch_shapes=scratch,
        compiler_params=pltpu.CompilerParams(
            collective_id=phase, has_side_effects=True, vmem_limit_bytes=(34 << 20, 16 << 20)[phase]
        ),
        name=("exchange_one", "exchange_two")[phase],
    )(*arrays)


def places(phase, source, target, sem):
    for c in range(CORES):
        rectangles = [(2 * pair, start, size) for pair, start, size in SHORT[c][phase]]
        rectangles += [(source.shape[1] - 2, start, size) for start, size in LONG[c][phase]]
        copies = []
        for i, (s, start, size) in enumerate(rectangles):
            here = (slice(None), pl.ds(s, 2), slice(None), pl.ds(start, size))
            copies.append(pltpu.make_async_copy(source.at[here], target.at[here], sem.at[i]))
        yield c, copies


def run_by_core(groups, others):
    core = lax.axis_index("domain") % CORES

    def all_of(copies):
        for copy in copies:
            copy.start()
        for copy in copies:
            copy.wait()

    for c, copies in groups:
        pl.when(core == c)(lambda c=c, copies=copies: all_of(others + copies))


MOST = max(len(SHORT[c][p]) + len(LONG[c][p]) for c in range(CORES) for p in range(2))


def middle_kernel(fresh, buddy, w_out, m_out, v_out, buddy_out, mark, sem, other_sem):
    mark[...] = jnp.zeros(mark.shape, F32)
    outs = enumerate((w_out, m_out, v_out))
    copies = [pltpu.make_async_copy(fresh.at[a], out, other_sem.at[a]) for a, out in outs]
    run_by_core(places(0, buddy, buddy_out, sem), copies)


def middle(fresh, buddy):
    one = jax.ShapeDtypeStruct(fresh.shape[1:], F32)
    return pl.pallas_call(
        middle_kernel,
        out_shape=(one, one, one, jax.ShapeDtypeStruct(buddy.shape, F32), pltpu.VMEM((STRIPE, 128), F32)),
        in_specs=[IN_VMEM] * 2,
        out_specs=(IN_HBM,) * 4 + (IN_VMEM,),
        scratch_shapes=[DMA((MOST,)), DMA((3,))],
        compiler_params=pltpu.CompilerParams(vmem_limit_bytes=1 << 20),
        name="middle",
    )(fresh, buddy)


def finish_kernel(buddy, parity, buddy_in, buddy_out, parity_out, sem, other_sem):
    copies = [pltpu.make_async_copy(parity, parity_out, other_sem.at[0])]
    run_by_core(places(1, buddy, buddy_out, sem), copies)


def finish(buddy, parity, buddy_out):
    return pl.pallas_call(
        finish_kernel,
        out_shape=(
            jax.ShapeDtypeStruct(buddy.shape, F32),
            jax.ShapeDtypeStruct(parity.shape, F32),
        ),
        in_specs=[IN_VMEM] * 2 + [IN_HBM],
        out_specs=(IN_HBM,) * 2,
        input_output_aliases={2: 0},
        scratch_shapes=[DMA((MOST,)), DMA((1,))],
        compiler_params=pltpu.CompilerParams(vmem_limit_bytes=1 << 20),
        name="finish",
    )(buddy, parity, buddy_out)


def shards(weight, moment1, moment2, gradient, owner_table, exponents):
    rows, width = weight.shape
    w, m, v = (a.reshape(rows // STRIPE, STRIPE, width) for a in (weight, moment1, moment2))
    held = (owner_table.T, exponents, w, m, v, gradient)
    held = [pltpu.with_memory_space_constraint(a, pltpu.HBM) for a in held]
    shape = w.shape
    fresh, buddy, part, cross = exchange(0, shape, *held)
    w, m, v, buddy_out, mark = middle(fresh, buddy)
    buddy, parity = exchange(1, shape, fresh, mark, part, cross)
    buddy, parity = finish(buddy, parity, buddy_out)
    buddy = jnp.transpose(buddy.reshape(3, rows, width), (1, 0, 2))
    parity = jnp.transpose(parity, (1, 0, 2))
    return (*(a.reshape(rows, width) for a in (w, m, v)), buddy, parity)


def solution(mesh):
    rows = P(("group", "domain"), None)
    blocks = P(("group", "domain"), None, None)
    return jax.shard_map(
        shards,
        mesh=mesh,
        in_specs=(rows, rows, rows, rows, P(), P()),
        out_specs=(rows, rows, rows, blocks, blocks),
        check_vma=False,
    )
```

```python
import jax
import jax.numpy as jnp
from jax import lax
from jax.experimental import pallas as pl
from jax.experimental.pallas import tpu as pltpu
from jax.sharding import PartitionSpec as P

beta_one = 0.9
beta_two = 0.95
learning_rate = 0.02
weight_decay = 0.1
epsilon = 1e-08
step_count = 100.0

MESH = pl.DeviceIdType.MESH
XS, ZS, YS, ZLS, CORES = 4, 4, 4, 2, 2
ZHS = ZS // ZLS
STRIPE = 8
LONG = (
    (((0, 512), (512, 1536), (2048, 1536)), ((3584, 1152), (4736, 1152), (5888, 1280))),
    (((0, 512), (512, 2304), (2816, 2304)), ((5120, 1024), (6144, 1024))),
)
SHORT = (
    (((0, 0, 512), (0, 512, 6656), (1, 0, 3584)), ((1, 3584, 3584), (2, 0, 7168))),
    (((0, 0, 512), (0, 512, 6656), (1, 0, 7168), (2, 0, 1024)), ((2, 1024, 6144),)),
)
F32 = jnp.float32
DMA = pltpu.SemaphoreType.DMA
IN_HBM = pl.BlockSpec(memory_space=pltpu.HBM)
IN_VMEM = pl.BlockSpec(memory_space=pltpu.VMEM)


def adamw(weight, moment1, moment2, gradient):
    grad_float = gradient.astype(F32)
    first = beta_one * moment1 + (1.0 - beta_one) * grad_float
    second = beta_two * moment2 + (1.0 - beta_two) * grad_float * grad_float
    correct_one = 1.0 - beta_one**step_count
    correct_two = 1.0 - beta_two**step_count
    scaled_second = second * (1.0 / correct_two)
    spread = scaled_second * lax.rsqrt(scaled_second) + epsilon
    step = first * (learning_rate / correct_one) / spread
    return (weight * (1.0 - learning_rate * weight_decay) - step, first, second)


def coefficient(stripe, exponent):
    bits = [(jnp.right_shift(exponent, i) & 1).astype(F32) for i in range(3)]
    point = 1.0 + (2.0 * stripe.astype(F32) - 7.0) / 32.0
    square = point * point
    fourth = square * square
    power = 1.0
    for bit, factor in zip(bits, (point, square, fourth)):
        power = power * (1.0 + bit * (factor - 1.0))
    return power


def same(a, b):
    gap = a - b
    return 1 - jnp.minimum(jnp.maximum(gap, -gap), 1)


def loading_kernel(
    owners_in, exponents_in, w_in, m_in, v_in, g_in, fresh, buddy_ref, part_ref, cross_ref,
    w, m, v, g, load_sem, *rest,
):
    last, width = w.shape[0] // 2 - 1, w.shape[2]
    cut = LONG[0][0][0][1]
    blocks = [(0, 0, cut), (last, 0, cut), (0, cut, width - cut), (last, cut, width - cut)]
    blocks += [(pair, 0, width) for pair in range(1, last)]

    def loads(b):
        pair, start, size = blocks[b]
        two, rows, columns = pl.ds(2 * pair, 2), pl.ds(2 * STRIPE * pair, 2 * STRIPE), pl.ds(start, size)
        ends = [(src.at[two, :, columns], dst.at[two, :, columns]) for src, dst in ((w_in, w), (m_in, m), (v_in, v))]
        ends.append((g_in.at[rows, columns], g.at[rows, columns]))
        return [pltpu.make_async_copy(*e, load_sem.at[b, i]) for i, e in enumerate(ends)]

    def update(b):
        pair, start, size = blocks[b]
        columns = pl.ds(start, size)
        for load in loads(b):
            load.wait()
        gradient = g[pl.ds(2 * STRIPE * pair, 2 * STRIPE), columns].astype(F32)
        for h in range(2):
            s = 2 * pair + h
            new = adamw(
                w[s, :, columns], m[s, :, columns], v[s, :, columns],
                gradient[h * STRIPE : (h + 1) * STRIPE],
            )
            for a in range(3):
                fresh[a, s, :, columns] = new[a]

    def start_loads():
        for b in range(len(blocks)):
            for load in loads(b):
                load.start()

    arrays = (fresh, buddy_ref, part_ref, cross_ref)
    exchange_kernel(0, arrays, rest, (start_loads, update, owners_in, exponents_in))


def second_kernel(fresh, after, part_ref, cross_ref, buddy_ref, parity_ref, *rest):
    exchange_kernel(1, (fresh, buddy_ref, part_ref, cross_ref), rest, parity_ref)


def exchange_kernel(phase, arrays, scratch, more):
    fresh, buddy_ref, part_ref, cross_ref = arrays
    hop1, hop2, plus_send, plus_recv, hop_send, hop_recv, ring_sem = scratch[:7]
    if phase == 0:
        start_loads, update, owners_in, exponents_in = more
        owner_ref, exponent_ref, scaled, first_in, second_in, table_sem, x_send, x_recv = scratch[7:]
    else:
        parity_ref = more
        relay, across, z_send, z_recv = scratch[7:]
    group = lax.axis_index("group")
    domain = lax.axis_index("domain")
    x, zh = group % XS, group // XS
    core, zl, y = domain % CORES, (domain // CORES) % ZLS, domain // (CORES * ZLS)
    z = zh * ZLS + zl

    def device(x, y, z):
        return ((z // ZLS) * XS + x, (y * ZLS + z % ZLS) * CORES + core)

    y_plus, y_minus = device(x, (y + 1) % YS, z), device(x, (y + YS - 1) % YS, z)
    x_plus, x_minus = device((x + 1) % XS, y, z), device((x + XS - 1) % XS, y, z)
    z_plus, z_minus = device(x, y, (z + 1) % ZS), device(x, y, (z + ZS - 1) % ZS)
    stripes = fresh.shape[1]
    half = fresh.shape[3] // 2
    last = stripes // 2 - 1

    if phase == 0:
        start_loads()

    def send(source, target, send_sem, recv_sem, to):
        return pltpu.make_async_remote_copy(
            src_ref=source,
            dst_ref=target,
            send_sem=send_sem,
            recv_sem=recv_sem,
            device_id=to,
            device_id_type=MESH,
        )

    barrier = pltpu.get_barrier_semaphore()

    def greet(*others, semaphore=barrier):
        for other in others:
            pl.semaphore_signal(semaphore, inc=1, device_id=other, device_id_type=MESH)

    greet(y_plus, y_minus)

    corner = y == 0
    beside = (x_plus, x_minus) if phase == 0 else ()

    @pl.when(corner)
    def _():
        greet(*beside)

        @pl.when(z < ZS - 1)
        def _():
            greet(z_plus)

        @pl.when(z > 0)
        def _():
            greet(z_minus)

    if phase == 0:
        update(0)

    @pl.when(jnp.logical_not(corner))
    def _():
        pl.semaphore_wait(barrier, 2)

    @pl.when(corner & (z == 0))
    def _():
        pl.semaphore_wait(barrier, 3 + len(beside))
        greet(z_minus)

    @pl.when(corner & (z > 0))
    def _():
        pl.semaphore_wait(barrier, 4 + len(beside))

    @pl.when(corner & (z == ZS - 1))
    def _():
        greet(z_plus)

    @pl.when(y == 1)
    def _():
        greet(y_minus, semaphore=ring_sem.at[0])

    def meet_the_rest():
        @pl.when((y == 0) & (z == 0))
        def _():
            pl.semaphore_wait(barrier, 1)

        @pl.when(y == 0)
        def _():
            pl.semaphore_wait(ring_sem.at[0], 1)
            greet(*beside, z_plus, z_minus, semaphore=ring_sem.at[1])
            pl.semaphore_wait(ring_sem.at[1], 2 + len(beside))
            greet(y_plus, y_minus, semaphore=ring_sem.at[2])

        @pl.when(y > 0)
        def _():
            pl.semaphore_wait(ring_sem.at[2], 1)

        @pl.when(y == 1)
        def _():
            greet(y_plus, semaphore=ring_sem.at[2])

    def short(c):
        copies = []
        for i, (pair, start, size) in enumerate(SHORT[c][phase]):
            here = (slice(None), pl.ds(2 * pair, 2), slice(None), pl.ds(start, size))
            copies.append(send(fresh.at[here], buddy_ref.at[here], plus_send.at[i], plus_recv.at[i], y_plus))
        return copies

    def hops(c, step):
        copies = []
        for i, (start, size) in enumerate(LONG[c][phase]):
            here = (slice(None), pl.ds(2 * last, 2), slice(None), pl.ds(start, size))
            held = (i, slice(None), slice(None), slice(None), pl.ds(0, size))
            source = (fresh.at[here], hop1.at[held], hop2.at[held])[step]
            target = (hop1.at[held], hop2.at[held], buddy_ref.at[here])[step]
            copies.append(send(source, target, hop_send.at[step, i], hop_recv.at[step, i], y_minus))
        return copies

    def by_core(act):
        for c in range(CORES):
            pl.when(core == c)(lambda c=c: act(c))

    def start_all(copies):
        for copy in copies:
            copy.start()

    def pass_on(c, step, chunks=slice(None)):
        for arrived, on in list(zip(hops(c, step), hops(c, step + 1)))[chunks]:
            arrived.wait_recv()
            on.start()

    def end(c):
        for step in range(3):
            for copy in hops(c, step):
                copy.wait_send()
        for copy in short(c):
            copy.wait()
        for copy in hops(c, 2):
            copy.wait_recv()

    if phase == 1:
        left, right = pl.ds(0, half), pl.ds(half, half)
        out_plus = send(cross_ref.at[:, :, left], relay.at[0], z_send.at[0], z_recv.at[0], z_plus)
        out_minus = send(cross_ref.at[:, :, right], relay.at[1], z_send.at[1], z_recv.at[1], z_minus)
        on_plus = send(relay.at[0], across.at[0], z_send.at[2], z_recv.at[2], z_plus)
        on_minus = send(relay.at[1], across.at[1], z_send.at[3], z_recv.at[3], z_minus)

        def totals():
            out_plus.wait_recv()
            on_plus.start()
            out_minus.wait_recv()
            on_minus.start()
            on_plus.wait_recv()
            parity_ref[:, :, left] = part_ref[:, :, left] + across[0]
            on_minus.wait_recv()
            parity_ref[:, :, right] = part_ref[:, :, right] + across[1]
            for copy in (out_plus, out_minus, on_plus, on_minus):
                copy.wait_send()

        def all_of(c):
            start_all(hops(c, 0) + short(c))
            pass_on(c, 0)
            meet_the_rest()
            out_plus.start()
            out_minus.start()
            pass_on(c, 1)
            totals()
            end(c)

        by_core(all_of)
        return

    tables = [
        pltpu.make_async_copy(owners_in, owner_ref, table_sem.at[0]),
        pltpu.make_async_copy(exponents_in, exponent_ref, table_sem.at[1]),
    ]
    by_core(lambda c: short(c)[0].start())
    start_all(tables)
    update(1)
    by_core(lambda c: hops(c, 0)[0].start())
    update(2)
    by_core(lambda c: short(c)[1].start())
    update(3)
    by_core(lambda c: start_all(hops(c, 0)[1:]))
    update(4)
    by_core(lambda c: short(c)[2].start())
    update(5)
    by_core(lambda c: start_all(short(c)[3:]))
    for table in tables:
        table.wait()
    meet_the_rest()

    def scale(dx, dz):
        owner = ((zh + dz) % ZHS) * XS + (x + dx) % XS
        stripe = jnp.int32(0)
        for s in range(stripes):
            stripe = stripe + s * same(owner_ref[s, domain], owner)
        stripe = jnp.minimum(stripe, stripes - 1)
        factor = coefficient(stripe, exponent_ref[group])
        for a in range(3):
            scaled[dz * XS + dx, a] = fresh[a, stripe] * factor

    def along_x(i, slot, target, to):
        return send(scaled.at[slot], target, x_send.at[i], x_recv.at[i], to)

    far_plus = along_x(0, 2, first_in.at[0], x_plus)
    far_minus = along_x(1, XS + 2, first_in.at[1], x_minus)
    near_plus = along_x(2, XS + 1, second_in.at[0], x_plus)
    near_minus = along_x(3, XS - 1, second_in.at[1], x_minus)
    sum_plus = along_x(4, 1, second_in.at[2], x_plus)
    sum_minus = along_x(5, XS + XS - 1, second_in.at[3], x_minus)
    def terms():
        scale(2, 0)
        far_plus.start()
        scale(2, 1)
        far_minus.start()
        scale(1, 1)
        near_plus.start()
        scale(3, 0)
        near_minus.start()
        scale(1, 0)
        scale(3, 1)
        scale(0, 0)
        scale(0, 1)

    def first_sums():
        far_plus.wait_recv()
        scaled[1] += first_in[0]
        sum_plus.start()
        far_minus.wait_recv()
        scaled[XS + XS - 1] += first_in[1]
        sum_minus.start()

    def sums():
        for copy in (near_plus, near_minus, sum_plus, sum_minus):
            copy.wait_recv()
        cross_ref[...] = scaled[XS] + second_in[0] + second_in[3]
        part_ref[...] = scaled[0] + second_in[1] + second_in[2]
        for copy in (far_plus, far_minus, near_plus, near_minus, sum_plus, sum_minus):
            copy.wait_send()

    @pl.when(core == 0)
    def _():
        terms()
        pass_on(0, 0)
        first_sums()
        pass_on(0, 1)
        sums()
        end(0)

    @pl.when(core == 1)
    def _():
        pass_on(1, 0)
        terms()
        pass_on(1, 1, slice(0, 2))
        first_sums()
        pass_on(1, 1, slice(2, None))
        sums()
        end(1)


def exchange(phase, shape, *arrays):
    stripes, _, width = shape
    block = (3, STRIPE, width)
    halves = (2, 3, STRIPE, width // 2)
    most_long = max(len(core[phase]) for core in LONG)
    most_short = max(len(core[phase]) for core in SHORT)
    held = (most_long, 3, 2, STRIPE, max(size for core in LONG for _, size in core[phase]))
    whole = pltpu.VMEM((3, *shape), F32)
    scratch = [pltpu.VMEM(held, F32)] * 2 + [DMA((most_short,))] * 2 + [DMA((3, most_long))] * 2
    scratch += [pltpu.SemaphoreType.REGULAR((3,))]
    if phase == 0:
        gradient = arrays[5]
        loaded = [pltpu.VMEM(shape, F32)] * 3 + [pltpu.VMEM(gradient.shape, gradient.dtype)]
        scratch = [*loaded, DMA((stripes // 2 + 2, 4)), *scratch]
        scratch += [
            pltpu.SMEM(arrays[0].shape, jnp.int32),
            pltpu.SMEM(arrays[1].shape, jnp.int32),
            pltpu.VMEM((XS * ZHS, *block), F32),
            pltpu.VMEM((2, *block), F32),
            pltpu.VMEM((4, *block), F32),
            DMA((2,)),
            DMA((6,)),
            DMA((6,)),
        ]
    else:
        scratch += [pltpu.VMEM(halves, F32)] * 2 + [DMA((4,))] * 2
    part = pltpu.VMEM(block, F32)
    return pl.pallas_call(
        (loading_kernel, second_kernel)[phase],
        out_shape=((whole, whole, part, part), (whole, part))[phase],
        in_specs=([IN_HBM] * 6, [IN_VMEM] * 4)[phase],
        out_specs=(IN_VMEM,) * (4, 2)[phase],
        scratch_shapes=scratch,
        compiler_params=pltpu.CompilerParams(
            collective_id=phase, has_side_effects=True, vmem_limit_bytes=(34 << 20, 16 << 20)[phase]
        ),
        name=("exchange_one", "exchange_two")[phase],
    )(*arrays)


def places(phase, source, target, sem):
    for c in range(CORES):
        rectangles = [(2 * pair, start, size) for pair, start, size in SHORT[c][phase]]
        rectangles += [(source.shape[1] - 2, start, size) for start, size in LONG[c][phase]]
        copies = []
        for i, (s, start, size) in enumerate(rectangles):
            here = (slice(None), pl.ds(s, 2), slice(None), pl.ds(start, size))
            copies.append(pltpu.make_async_copy(source.at[here], target.at[here], sem.at[i]))
        yield c, copies


def run_by_core(groups, others):
    core = lax.axis_index("domain") % CORES

    def all_of(copies):
        for copy in copies:
            copy.start()
        for copy in copies:
            copy.wait()

    for c, copies in groups:
        pl.when(core == c)(lambda c=c, copies=copies: all_of(others + copies))


MOST = max(len(SHORT[c][p]) + len(LONG[c][p]) for c in range(CORES) for p in range(2))


def middle_kernel(fresh, buddy, w_out, m_out, v_out, buddy_out, mark, sem, other_sem):
    mark[...] = jnp.zeros(mark.shape, F32)
    outs = enumerate((w_out, m_out, v_out))
    copies = [pltpu.make_async_copy(fresh.at[a], out, other_sem.at[a]) for a, out in outs]
    run_by_core(places(0, buddy, buddy_out, sem), copies)


def middle(fresh, buddy):
    one = jax.ShapeDtypeStruct(fresh.shape[1:], F32)
    return pl.pallas_call(
        middle_kernel,
        out_shape=(one, one, one, jax.ShapeDtypeStruct(buddy.shape, F32), pltpu.VMEM((STRIPE, 128), F32)),
        in_specs=[IN_VMEM] * 2,
        out_specs=(IN_HBM,) * 4 + (IN_VMEM,),
        scratch_shapes=[DMA((MOST,)), DMA((3,))],
        compiler_params=pltpu.CompilerParams(vmem_limit_bytes=1 << 20),
        name="middle",
    )(fresh, buddy)


def finish_kernel(buddy, parity, buddy_in, buddy_out, parity_out, sem, other_sem):
    copies = [pltpu.make_async_copy(parity, parity_out, other_sem.at[0])]
    run_by_core(places(1, buddy, buddy_out, sem), copies)


def finish(buddy, parity, buddy_out):
    return pl.pallas_call(
        finish_kernel,
        out_shape=(
            jax.ShapeDtypeStruct(buddy.shape, F32),
            jax.ShapeDtypeStruct(parity.shape, F32),
        ),
        in_specs=[IN_VMEM] * 2 + [IN_HBM],
        out_specs=(IN_HBM,) * 2,
        input_output_aliases={2: 0},
        scratch_shapes=[DMA((MOST,)), DMA((1,))],
        compiler_params=pltpu.CompilerParams(vmem_limit_bytes=1 << 20),
        name="finish",
    )(buddy, parity, buddy_out)


def shards(weight, moment1, moment2, gradient, owner_table, exponents):
    rows, width = weight.shape
    w, m, v = (a.reshape(rows // STRIPE, STRIPE, width) for a in (weight, moment1, moment2))
    held = (owner_table.T, exponents, w, m, v, gradient)
    held = [pltpu.with_memory_space_constraint(a, pltpu.HBM) for a in held]
    shape = w.shape
    fresh, buddy, part, cross = exchange(0, shape, *held)
    w, m, v, buddy_out, mark = middle(fresh, buddy)
    buddy, parity = exchange(1, shape, fresh, mark, part, cross)
    buddy, parity = finish(buddy, parity, buddy_out)
    buddy = jnp.transpose(buddy.reshape(3, rows, width), (1, 0, 2))
    parity = jnp.transpose(parity, (1, 0, 2))
    return (*(a.reshape(rows, width) for a in (w, m, v)), buddy, parity)


def solution(mesh):
    rows = P(("group", "domain"), None)
    blocks = P(("group", "domain"), None, None)
    return jax.shard_map(
        shards,
        mesh=mesh,
        in_specs=(rows, rows, rows, rows, P(), P()),
        out_specs=(rows, rows, rows, blocks, blocks),
        check_vma=False,
    )
```

```python
import jax
import jax.numpy as jnp
from jax import lax
from jax.experimental import pallas as pl
from jax.experimental.pallas import tpu as pltpu
from jax.sharding import PartitionSpec as P

beta_one = 0.9
beta_two = 0.95
learning_rate = 0.02
weight_decay = 0.1
epsilon = 1e-08
step_count = 100.0

MESH = pl.DeviceIdType.MESH
XS, ZS, YS, ZLS, CORES = 4, 4, 4, 2, 2
ZHS = ZS // ZLS
STRIPE = 8
LONG = (
    (((0, 512), (512, 1536), (2048, 1536)), ((3584, 1152), (4736, 1152), (5888, 1280))),
    (((0, 512), (512, 2304), (2816, 2304)), ((5120, 1024), (6144, 1024))),
)
SHORT = (
    (((0, 0, 512), (0, 512, 6656), (1, 0, 3584)), ((1, 3584, 3584), (2, 0, 3584), (2, 3584, 3584))),
    (((0, 0, 512), (0, 512, 6656), (1, 0, 7168), (2, 0, 1024)), ((2, 1024, 3072), (2, 4096, 3072))),
)
F32 = jnp.float32
DMA = pltpu.SemaphoreType.DMA
IN_HBM = pl.BlockSpec(memory_space=pltpu.HBM)
IN_VMEM = pl.BlockSpec(memory_space=pltpu.VMEM)


def adamw(weight, moment1, moment2, gradient):
    grad_float = gradient.astype(F32)
    first = beta_one * moment1 + (1.0 - beta_one) * grad_float
    second = beta_two * moment2 + (1.0 - beta_two) * grad_float * grad_float
    correct_one = 1.0 - beta_one**step_count
    correct_two = 1.0 - beta_two**step_count
    scaled_second = second * (1.0 / correct_two)
    spread = scaled_second * lax.rsqrt(scaled_second) + epsilon
    step = first * (learning_rate / correct_one) / spread
    return (weight * (1.0 - learning_rate * weight_decay) - step, first, second)


def coefficient(stripe, exponent):
    bits = [(jnp.right_shift(exponent, i) & 1).astype(F32) for i in range(3)]
    point = 1.0 + (2.0 * stripe.astype(F32) - 7.0) / 32.0
    square = point * point
    fourth = square * square
    power = 1.0
    for bit, factor in zip(bits, (point, square, fourth)):
        power = power * (1.0 + bit * (factor - 1.0))
    return power


def same(a, b):
    gap = a - b
    return 1 - jnp.minimum(jnp.maximum(gap, -gap), 1)


def loading_kernel(
    owners_in, exponents_in, w_in, m_in, v_in, g_in, fresh, buddy_ref, part_ref, cross_ref,
    w, m, v, g, load_sem, *rest,
):
    last, width = w.shape[0] // 2 - 1, w.shape[2]
    cut = LONG[0][0][0][1]
    blocks = [(0, 0, cut), (last, 0, cut), (0, cut, width - cut), (last, cut, width - cut)]
    blocks += [(pair, 0, width) for pair in range(1, last)]

    def loads(b):
        pair, start, size = blocks[b]
        two, rows, columns = pl.ds(2 * pair, 2), pl.ds(2 * STRIPE * pair, 2 * STRIPE), pl.ds(start, size)
        ends = [(src.at[two, :, columns], dst.at[two, :, columns]) for src, dst in ((w_in, w), (m_in, m), (v_in, v))]
        ends.append((g_in.at[rows, columns], g.at[rows, columns]))
        return [pltpu.make_async_copy(*e, load_sem.at[b, i]) for i, e in enumerate(ends)]

    def update(b):
        pair, start, size = blocks[b]
        columns = pl.ds(start, size)
        for load in loads(b):
            load.wait()
        gradient = g[pl.ds(2 * STRIPE * pair, 2 * STRIPE), columns].astype(F32)
        for h in range(2):
            s = 2 * pair + h
            new = adamw(
                w[s, :, columns], m[s, :, columns], v[s, :, columns],
                gradient[h * STRIPE : (h + 1) * STRIPE],
            )
            for a in range(3):
                fresh[a, s, :, columns] = new[a]

    def start_loads():
        for b in range(len(blocks)):
            for load in loads(b):
                load.start()

    arrays = (fresh, buddy_ref, part_ref, cross_ref)
    exchange_kernel(0, arrays, rest, (start_loads, update, owners_in, exponents_in))


def second_kernel(fresh, after, part_ref, cross_ref, buddy_ref, parity_ref, *rest):
    exchange_kernel(1, (fresh, buddy_ref, part_ref, cross_ref), rest, parity_ref)


def exchange_kernel(phase, arrays, scratch, more):
    fresh, buddy_ref, part_ref, cross_ref = arrays
    hop1, hop2, plus_send, plus_recv, hop_send, hop_recv, ring_sem = scratch[:7]
    if phase == 0:
        start_loads, update, owners_in, exponents_in = more
        owner_ref, exponent_ref, scaled, first_in, second_in, table_sem, x_send, x_recv = scratch[7:]
    else:
        parity_ref = more
        relay, across, z_send, z_recv = scratch[7:]
    group = lax.axis_index("group")
    domain = lax.axis_index("domain")
    x, zh = group % XS, group // XS
    core, zl, y = domain % CORES, (domain // CORES) % ZLS, domain // (CORES * ZLS)
    z = zh * ZLS + zl

    def device(x, y, z):
        return ((z // ZLS) * XS + x, (y * ZLS + z % ZLS) * CORES + core)

    y_plus, y_minus = device(x, (y + 1) % YS, z), device(x, (y + YS - 1) % YS, z)
    x_plus, x_minus = device((x + 1) % XS, y, z), device((x + XS - 1) % XS, y, z)
    z_plus, z_minus = device(x, y, (z + 1) % ZS), device(x, y, (z + ZS - 1) % ZS)
    stripes = fresh.shape[1]
    half = fresh.shape[3] // 2
    last = stripes // 2 - 1

    if phase == 0:
        start_loads()

    def send(source, target, send_sem, recv_sem, to):
        return pltpu.make_async_remote_copy(
            src_ref=source,
            dst_ref=target,
            send_sem=send_sem,
            recv_sem=recv_sem,
            device_id=to,
            device_id_type=MESH,
        )

    barrier = pltpu.get_barrier_semaphore()

    def greet(*others, semaphore=barrier):
        for other in others:
            pl.semaphore_signal(semaphore, inc=1, device_id=other, device_id_type=MESH)

    greet(y_plus, y_minus)

    corner = y == 0

    @pl.when(corner)
    def _():
        greet(x_plus, x_minus)

        @pl.when(z < ZS - 1)
        def _():
            greet(z_plus)

        @pl.when(z > 0)
        def _():
            greet(z_minus)

    if phase == 0:
        update(0)

    @pl.when(jnp.logical_not(corner))
    def _():
        pl.semaphore_wait(barrier, 2)

    @pl.when(corner & (z == 0))
    def _():
        pl.semaphore_wait(barrier, 5)
        greet(z_minus)

    @pl.when(corner & (z > 0))
    def _():
        pl.semaphore_wait(barrier, 6)

    @pl.when(corner & (z == ZS - 1))
    def _():
        greet(z_plus)

    @pl.when(y == 1)
    def _():
        greet(y_minus, semaphore=ring_sem.at[0])

    def meet_the_rest():
        @pl.when((y == 0) & (z == 0))
        def _():
            pl.semaphore_wait(barrier, 1)

        @pl.when(y == 0)
        def _():
            pl.semaphore_wait(ring_sem.at[0], 1)
            greet(x_plus, x_minus, z_plus, z_minus, semaphore=ring_sem.at[1])
            pl.semaphore_wait(ring_sem.at[1], 4)
            greet(y_plus, y_minus, semaphore=ring_sem.at[2])

        @pl.when(y > 0)
        def _():
            pl.semaphore_wait(ring_sem.at[2], 1)

        @pl.when(y == 1)
        def _():
            greet(y_plus, semaphore=ring_sem.at[2])

    def short(c):
        copies = []
        for i, (pair, start, size) in enumerate(SHORT[c][phase]):
            here = (slice(None), pl.ds(2 * pair, 2), slice(None), pl.ds(start, size))
            copies.append(send(fresh.at[here], buddy_ref.at[here], plus_send.at[i], plus_recv.at[i], y_plus))
        return copies

    def hops(c, step):
        copies = []
        for i, (start, size) in enumerate(LONG[c][phase]):
            here = (slice(None), pl.ds(2 * last, 2), slice(None), pl.ds(start, size))
            held = (i, slice(None), slice(None), slice(None), pl.ds(0, size))
            source = (fresh.at[here], hop1.at[held], hop2.at[held])[step]
            target = (hop1.at[held], hop2.at[held], buddy_ref.at[here])[step]
            copies.append(send(source, target, hop_send.at[step, i], hop_recv.at[step, i], y_minus))
        return copies

    def by_core(act):
        for c in range(CORES):
            pl.when(core == c)(lambda c=c: act(c))

    def start_all(copies):
        for copy in copies:
            copy.start()

    def pass_on(c, step, chunks=slice(None)):
        for arrived, on in list(zip(hops(c, step), hops(c, step + 1)))[chunks]:
            arrived.wait_recv()
            on.start()

    def end(c):
        for step in range(3):
            for copy in hops(c, step):
                copy.wait_send()
        for copy in short(c):
            copy.wait()
        for copy in hops(c, 2):
            copy.wait_recv()

    if phase == 1:
        left, right = pl.ds(0, half), pl.ds(half, half)
        out_plus = send(cross_ref.at[:, :, left], relay.at[0], z_send.at[0], z_recv.at[0], z_plus)
        out_minus = send(cross_ref.at[:, :, right], relay.at[1], z_send.at[1], z_recv.at[1], z_minus)
        on_plus = send(relay.at[0], across.at[0], z_send.at[2], z_recv.at[2], z_plus)
        on_minus = send(relay.at[1], across.at[1], z_send.at[3], z_recv.at[3], z_minus)

        def totals():
            out_plus.wait_recv()
            on_plus.start()
            out_minus.wait_recv()
            on_minus.start()
            on_plus.wait_recv()
            parity_ref[:, :, left] = part_ref[:, :, left] + across[0]
            on_minus.wait_recv()
            parity_ref[:, :, right] = part_ref[:, :, right] + across[1]
            for copy in (out_plus, out_minus, on_plus, on_minus):
                copy.wait_send()

        def all_of(c):
            start_all(hops(c, 0) + short(c))
            meet_the_rest()
            out_plus.start()
            out_minus.start()
            pass_on(c, 0)
            pass_on(c, 1)
            totals()
            end(c)

        by_core(all_of)
        return

    tables = [
        pltpu.make_async_copy(owners_in, owner_ref, table_sem.at[0]),
        pltpu.make_async_copy(exponents_in, exponent_ref, table_sem.at[1]),
    ]
    by_core(lambda c: short(c)[0].start())
    start_all(tables)
    update(1)
    by_core(lambda c: hops(c, 0)[0].start())
    update(2)
    by_core(lambda c: short(c)[1].start())
    update(3)
    by_core(lambda c: start_all(hops(c, 0)[1:]))
    update(4)
    by_core(lambda c: short(c)[2].start())
    update(5)
    by_core(lambda c: start_all(short(c)[3:]))
    for table in tables:
        table.wait()
    meet_the_rest()

    def scale(dx, dz):
        owner = ((zh + dz) % ZHS) * XS + (x + dx) % XS
        stripe = jnp.int32(0)
        for s in range(stripes):
            stripe = stripe + s * same(owner_ref[s, domain], owner)
        stripe = jnp.minimum(stripe, stripes - 1)
        factor = coefficient(stripe, exponent_ref[group])
        for a in range(3):
            scaled[dz * XS + dx, a] = fresh[a, stripe] * factor

    def along_x(i, slot, target, to):
        return send(scaled.at[slot], target, x_send.at[i], x_recv.at[i], to)

    far_plus = along_x(0, 2, first_in.at[0], x_plus)
    far_minus = along_x(1, XS + 2, first_in.at[1], x_minus)
    near_plus = along_x(2, XS + 1, second_in.at[0], x_plus)
    near_minus = along_x(3, XS - 1, second_in.at[1], x_minus)
    sum_plus = along_x(4, 1, second_in.at[2], x_plus)
    sum_minus = along_x(5, XS + XS - 1, second_in.at[3], x_minus)
    def terms():
        scale(2, 0)
        far_plus.start()
        scale(2, 1)
        far_minus.start()
        scale(1, 1)
        near_plus.start()
        scale(3, 0)
        near_minus.start()
        scale(1, 0)
        scale(3, 1)
        scale(0, 0)
        scale(0, 1)

    def first_sums():
        far_plus.wait_recv()
        scaled[1] += first_in[0]
        sum_plus.start()
        far_minus.wait_recv()
        scaled[XS + XS - 1] += first_in[1]
        sum_minus.start()

    def sums():
        for copy in (near_plus, near_minus, sum_plus, sum_minus):
            copy.wait_recv()
        cross_ref[...] = scaled[XS] + second_in[0] + second_in[3]
        part_ref[...] = scaled[0] + second_in[1] + second_in[2]
        for copy in (far_plus, far_minus, near_plus, near_minus, sum_plus, sum_minus):
            copy.wait_send()

    @pl.when(core == 0)
    def _():
        terms()
        pass_on(0, 0)
        first_sums()
        pass_on(0, 1)
        sums()
        end(0)

    @pl.when(core == 1)
    def _():
        pass_on(1, 0)
        terms()
        pass_on(1, 1, slice(0, 2))
        first_sums()
        pass_on(1, 1, slice(2, None))
        sums()
        end(1)


def exchange(phase, shape, *arrays):
    stripes, _, width = shape
    block = (3, STRIPE, width)
    halves = (2, 3, STRIPE, width // 2)
    most_long = max(len(core[phase]) for core in LONG)
    most_short = max(len(core[phase]) for core in SHORT)
    held = (most_long, 3, 2, STRIPE, max(size for core in LONG for _, size in core[phase]))
    whole = pltpu.VMEM((3, *shape), F32)
    scratch = [pltpu.VMEM(held, F32)] * 2 + [DMA((most_short,))] * 2 + [DMA((3, most_long))] * 2
    scratch += [pltpu.SemaphoreType.REGULAR((3,))]
    if phase == 0:
        gradient = arrays[5]
        loaded = [pltpu.VMEM(shape, F32)] * 3 + [pltpu.VMEM(gradient.shape, gradient.dtype)]
        scratch = [*loaded, DMA((stripes // 2 + 2, 4)), *scratch]
        scratch += [
            pltpu.SMEM(arrays[0].shape, jnp.int32),
            pltpu.SMEM(arrays[1].shape, jnp.int32),
            pltpu.VMEM((XS * ZHS, *block), F32),
            pltpu.VMEM((2, *block), F32),
            pltpu.VMEM((4, *block), F32),
            DMA((2,)),
            DMA((6,)),
            DMA((6,)),
        ]
    else:
        scratch += [pltpu.VMEM(halves, F32)] * 2 + [DMA((4,))] * 2
    part = pltpu.VMEM(block, F32)
    return pl.pallas_call(
        (loading_kernel, second_kernel)[phase],
        out_shape=((whole, whole, part, part), (whole, part))[phase],
        in_specs=([IN_HBM] * 6, [IN_VMEM] * 4)[phase],
        out_specs=(IN_VMEM,) * (4, 2)[phase],
        scratch_shapes=scratch,
        compiler_params=pltpu.CompilerParams(
            collective_id=phase, has_side_effects=True, vmem_limit_bytes=(34 << 20, 16 << 20)[phase]
        ),
        name=("exchange_one", "exchange_two")[phase],
    )(*arrays)


def places(phase, source, target, sem):
    for c in range(CORES):
        rectangles = [(2 * pair, start, size) for pair, start, size in SHORT[c][phase]]
        rectangles += [(source.shape[1] - 2, start, size) for start, size in LONG[c][phase]]
        copies = []
        for i, (s, start, size) in enumerate(rectangles):
            here = (slice(None), pl.ds(s, 2), slice(None), pl.ds(start, size))
            copies.append(pltpu.make_async_copy(source.at[here], target.at[here], sem.at[i]))
        yield c, copies


def run_by_core(groups, others):
    core = lax.axis_index("domain") % CORES

    def all_of(copies):
        for copy in copies:
            copy.start()
        for copy in copies:
            copy.wait()

    for c, copies in groups:
        pl.when(core == c)(lambda c=c, copies=copies: all_of(others + copies))


MOST = max(len(SHORT[c][p]) + len(LONG[c][p]) for c in range(CORES) for p in range(2))


def middle_kernel(fresh, buddy, w_out, m_out, v_out, buddy_out, mark, sem, other_sem):
    mark[...] = jnp.zeros(mark.shape, F32)
    outs = enumerate((w_out, m_out, v_out))
    copies = [pltpu.make_async_copy(fresh.at[a], out, other_sem.at[a]) for a, out in outs]
    run_by_core(places(0, buddy, buddy_out, sem), copies)


def middle(fresh, buddy):
    one = jax.ShapeDtypeStruct(fresh.shape[1:], F32)
    return pl.pallas_call(
        middle_kernel,
        out_shape=(one, one, one, jax.ShapeDtypeStruct(buddy.shape, F32), pltpu.VMEM((STRIPE, 128), F32)),
        in_specs=[IN_VMEM] * 2,
        out_specs=(IN_HBM,) * 4 + (IN_VMEM,),
        scratch_shapes=[DMA((MOST,)), DMA((3,))],
        compiler_params=pltpu.CompilerParams(vmem_limit_bytes=1 << 20),
        name="middle",
    )(fresh, buddy)


def finish_kernel(buddy, parity, buddy_in, buddy_out, parity_out, sem, other_sem):
    copies = [pltpu.make_async_copy(parity, parity_out, other_sem.at[0])]
    run_by_core(places(1, buddy, buddy_out, sem), copies)


def finish(buddy, parity, buddy_out):
    return pl.pallas_call(
        finish_kernel,
        out_shape=(
            jax.ShapeDtypeStruct(buddy.shape, F32),
            jax.ShapeDtypeStruct(parity.shape, F32),
        ),
        in_specs=[IN_VMEM] * 2 + [IN_HBM],
        out_specs=(IN_HBM,) * 2,
        input_output_aliases={2: 0},
        scratch_shapes=[DMA((MOST,)), DMA((1,))],
        compiler_params=pltpu.CompilerParams(vmem_limit_bytes=1 << 20),
        name="finish",
    )(buddy, parity, buddy_out)


def shards(weight, moment1, moment2, gradient, owner_table, exponents):
    rows, width = weight.shape
    w, m, v = (a.reshape(rows // STRIPE, STRIPE, width) for a in (weight, moment1, moment2))
    held = (owner_table.T, exponents, w, m, v, gradient)
    held = [pltpu.with_memory_space_constraint(a, pltpu.HBM) for a in held]
    shape = w.shape
    fresh, buddy, part, cross = exchange(0, shape, *held)
    w, m, v, buddy_out, mark = middle(fresh, buddy)
    buddy, parity = exchange(1, shape, fresh, mark, part, cross)
    buddy, parity = finish(buddy, parity, buddy_out)
    buddy = jnp.transpose(buddy.reshape(3, rows, width), (1, 0, 2))
    parity = jnp.transpose(parity, (1, 0, 2))
    return (*(a.reshape(rows, width) for a in (w, m, v)), buddy, parity)


def solution(mesh):
    rows = P(("group", "domain"), None)
    blocks = P(("group", "domain"), None, None)
    return jax.shard_map(
        shards,
        mesh=mesh,
        in_specs=(rows, rows, rows, rows, P(), P()),
        out_specs=(rows, rows, rows, blocks, blocks),
        check_vma=False,
    )
```
